32 devices in a mesh: seq: 8 (over z, x), head: 4 (over y, core).
Axes of the slice: x: 2, y: 2, z: 4, core: 2. Of those that a mesh axis runs over, the one named last changes fastest.
Arguments:
- layer_input: bfloat16 [1024, 8192], P('seq'), may hold values from -6 to 6
- beta_weight: bfloat16 [32, 8192], P('head'), may hold values from -0.0625 to 0.0625
- decay_weight: bfloat16 [32, 8192], P('head'), may hold values from -0.0625 to 0.0625
- log_rate: float32 [32], P('head'), may hold values from -11.5 to -3
- decay_bias: float32 [32], P('head'), may hold values from -2 to 1
- delta_query: bfloat16 [1024, 4096], P('seq', 'head'), may hold values from -6 to 6
- delta_key: bfloat16 [1024, 4096], P('seq', 'head'), may hold values from -6 to 6
- delta_value: bfloat16 [1024, 4096], P('seq', 'head'), may hold values from -6 to 6
- delta_out_grad: bfloat16 [1024, 4096], P('seq', 'head'), may hold values from -6 to 6
- state_init: float32 [32, 128, 128], P('head'), may hold values from -6 to 6
- state_grad_next: float32 [32, 128, 128], P('head'), may hold values from -6 to 6
- attn_query: bfloat16 [1024, 1024], P('seq', 'head'), may hold values from -80 to 80
- attn_key: bfloat16 [1024, 1024], P('seq', 'head'), may hold values from -12 to 12
- attn_value: bfloat16 [1024, 1024], P('seq', 'head'), may hold values from -6 to 6
- attn_out_grad: bfloat16 [1024, 1024], P('seq', 'head'), may hold values from -6 to 6
Outputs:
- delta_query_grad: float32 [1024, 4096], P('seq', 'head')
- delta_key_grad: float32 [1024, 4096], P('seq', 'head')
- delta_value_grad: float32 [1024, 4096], P('seq', 'head')
- boundary_grads: float32 [8, 32, 128, 128], P('seq', 'head')
- input_grad: float32 [1024, 8192], P('seq', 'head')
- beta_weight_grad: float32 [32, 8192], P('head', 'seq')
- decay_weight_grad: float32 [32, 8192], P('head', 'seq')
- log_rate_grad: float32 [32], P('head')
- decay_bias_grad: float32 [32], P('head')
- attn_query_grad: float32 [1024, 1024], P('seq', 'head')
- attn_key_grad: float32 [1024, 1024], P('seq', 'head')
- attn_value_grad: float32 [1024, 1024], P('seq', 'head')
The draws below stay inside these ranges and needn't reach their ends.
All inputs are finite; a program needn't handle non-finite values.
Results may differ from the reference program's by a relative error of at most 0.00035.
Values may be sent and summed in bfloat16 or wider, within the bound.
A program may use at most 128 MiB of HBM per device.

```python
import math
import jax
import jax.numpy as jnp
from jax import lax

D = 8192
HEADS = 32
DK = 128
DV = 128
STRETCH = 64
AHEADS = 8
AHD = 128
WINDOW = 1024
TOK_DEV = 128
TOKENS = 1024
N_SEQ = 8


def attention_pair(key):
    first_key, second_key = jax.random.split(jax.random.fold_in(key, 7))
    row_width = AHEADS * AHD
    queries = jnp.clip(jax.random.normal(first_key, (TOKENS, row_width), jnp.float32), -6.0, 6.0)
    key_rows = jnp.clip(jax.random.normal(second_key, (TOKENS, row_width), jnp.float32), -6.0, 6.0)
    return (queries, key_rows)


def draw_attn_query(key, part):
    return attention_pair(key)[0].astype(jnp.bfloat16)


def draw_attn_key(key, part):
    return attention_pair(key)[1].astype(jnp.bfloat16)


def draw_log_rate(key, part):
    slow_key, fast_key, pick_key = jax.random.split(jax.random.fold_in(key, 11), 3)
    slow = jax.random.uniform(slow_key, (HEADS,), jnp.float32, -11.5, -9.5)
    fast = jax.random.uniform(fast_key, (HEADS,), jnp.float32, -7.0, -3.0)
    share = 0.5
    picked = jax.random.uniform(pick_key, (HEADS,), jnp.float32) < share
    return jnp.where(picked, slow, fast)


def draw_delta_key(key, part):
    base_key, perm_key = jax.random.split(jax.random.fold_in(key, 13))
    base = jnp.clip(jax.random.normal(base_key, (TOKENS, HEADS, DK), jnp.float32), -6.0, 6.0)
    head_keys = jax.random.split(perm_key, HEADS)
    orders = jax.vmap(lambda one_key: jax.random.permutation(one_key, DK))(head_keys)
    inside = orders < max(DK // 8, 2)
    scales = jnp.where(inside, 1.0, 0.05).astype(jnp.float32)
    return (base * scales[None]).reshape(TOKENS, HEADS * DK).astype(jnp.bfloat16)


def level_of(rng, dims, cuts, smallest, high):
    gain, own = 1.0, jax.random.fold_in(rng, 6)
    for position, shards_of in cuts:
        heights = jnp.exp(jax.random.uniform(jax.random.fold_in(own, position), (shards_of,), jnp.float32, smallest / len(cuts), high / len(cuts)))
        gain = gain * jnp.repeat(heights, dims[position] // shards_of).reshape([-1 if axis == position else 1 for axis in range(len(dims))])
    return gain


def gaussian(own_key, extent, scale, limit, shards=(), kind=jnp.bfloat16):
    array = jax.random.normal(own_key, extent, jnp.float32) * scale
    if len(shards) > 0:
        array = level_of(own_key, extent, shards, -0.22, 0.18) * array
    return jnp.clip(array, min=-limit, max=limit).astype(kind)


def setup_inputs(seed: int = 0) -> dict:
    seeds = jax.random.split(jax.random.key(seed), 16)
    layer_input = gaussian(seeds[0], (TOKENS, D), 1.0, 6.0, ((0, 8),))
    beta_weight = gaussian(seeds[1], (HEADS, D), D ** -0.5, 0.0625, ((0, 4),))
    decay_weight = gaussian(seeds[2], (HEADS, D), D ** -0.5, 0.0625, ((0, 4),))
    log_rate = draw_log_rate(jax.random.fold_in(seeds[15], 71), 0)
    decay_bias = jnp.clip(-2.0 + 3.0 * jax.random.uniform(seeds[4], (HEADS,), jnp.float32) ** level_of(seeds[4], (HEADS,), ((0, 4),), -0.2, 0.2), -2.0, 1.0)
    delta_query = gaussian(seeds[5], (TOKENS, HEADS * DK), 1.0, 6.0, ((0, 8), (1, 4)))
    delta_key = draw_delta_key(jax.random.fold_in(seeds[15], 71), 0)
    delta_value = gaussian(seeds[7], (TOKENS, HEADS * DV), 1.0, 6.0, ((0, 8), (1, 4)))
    delta_out_grad = gaussian(seeds[8], (TOKENS, HEADS * DV), 1.0, 6.0, ((0, 8), (1, 4)))
    state_init = gaussian(seeds[9], (HEADS, DK, DV), 1.0, 6.0, ((0, 4),), jnp.float32)
    state_grad_next = gaussian(seeds[10], (HEADS, DK, DV), 1.0, 6.0, ((0, 4),), jnp.float32)
    attn_query = draw_attn_query(jax.random.fold_in(seeds[15], 71), 0)
    attn_key = draw_attn_key(jax.random.fold_in(seeds[15], 71), 0)
    attn_value = gaussian(seeds[13], (TOKENS, AHEADS * AHD), 1.0, 6.0, ((0, 8), (1, 4)))
    attn_out_grad = gaussian(seeds[14], (TOKENS, AHEADS * AHD), 1.0, 6.0, ((0, 8), (1, 4)))
    return {"layer_input": layer_input, "beta_weight": beta_weight, "decay_weight": decay_weight, "log_rate": log_rate, "decay_bias": decay_bias, "delta_query": delta_query, "delta_key": delta_key, "delta_value": delta_value, "delta_out_grad": delta_out_grad, "state_init": state_init, "state_grad_next": state_grad_next, "attn_query": attn_query, "attn_key": attn_key, "attn_value": attn_value, "attn_out_grad": attn_out_grad}


PRECISE = lax.Precision.HIGHEST

def dot_high(left_mat, right_mat):
    return jnp.matmul(left_mat, right_mat, precision=PRECISE)

def unit_rows(values):
    return values * lax.rsqrt(lax.optimization_barrier(jnp.sum(values * values, axis=-1, keepdims=True)) + 1e-06)

def stretch_step(memory, queries, key_rows, values, beta_rows, decay_log):
    span_len = queries.shape[0]
    cumulative = jnp.cumsum(decay_log)
    row_ids = lax.broadcasted_iota(jnp.int32, (span_len, span_len), 0)
    col_ids = lax.broadcasted_iota(jnp.int32, (span_len, span_len), 1)
    lower_mask = row_ids >= col_ids
    strict_mask = row_ids > col_ids
    ratios = jnp.where(lower_mask, jnp.exp(jnp.where(lower_mask, cumulative[:, None] - cumulative[None, :], 0.0)), 0.0)
    gram_keys = dot_high(key_rows, key_rows.T)
    system_mat = jnp.eye(span_len, dtype=queries.dtype) + jnp.where(strict_mask, beta_rows[:, None] * ratios * gram_keys, 0.0)
    growths = jnp.exp(cumulative)
    right_side = beta_rows[:, None] * (values - growths[:, None] * dot_high(key_rows, memory))
    updates = jax.scipy.linalg.solve_triangular(system_mat, right_side, lower=True, unit_diagonal=True)
    output = growths[:, None] * dot_high(queries, memory) + dot_high(ratios * dot_high(queries, key_rows.T), updates)
    tail_decay = jnp.exp(cumulative[-1] - cumulative)
    new_memory = jnp.exp(cumulative[-1]) * memory + dot_high((key_rows * tail_decay[:, None]).T, updates)
    return (new_memory, output)

def block_forward(memory, q_raw, k_raw, values, beta_rows, decay_rows):
    head_count, tok_count, key_width = q_raw.shape
    span_count = tok_count // STRETCH
    queries = unit_rows(q_raw) / math.sqrt(key_width)
    key_rows = unit_rows(k_raw)

    def in_stretches(array_in):
        return jnp.swapaxes(array_in.reshape((head_count, span_count, STRETCH) + array_in.shape[2:]), 0, 1)
    pieces_all = (in_stretches(queries), in_stretches(key_rows), in_stretches(values), in_stretches(beta_rows), in_stretches(decay_rows))
    stepper = jax.vmap(stretch_step)

    def advance(carried, pieces):
        return stepper(carried, pieces[0], pieces[1], pieces[2], pieces[3], pieces[4])
    final_mem, outputs = lax.scan(advance, memory, pieces_all)
    outputs = jnp.swapaxes(outputs, 0, 1).reshape(head_count, tok_count, values.shape[2])
    return (outputs, final_mem)

def gate_values(beta_logit, decay_input, log_rate, decay_bias):
    betas = jax.nn.sigmoid(beta_logit)
    decays = -jnp.exp(log_rate)[None, :] * jax.nn.softplus(decay_input + decay_bias[None, :])
    return (betas, decays)

def heads_first(flat_rows, head_count):
    return jnp.swapaxes(flat_rows.reshape(flat_rows.shape[0], head_count, -1), 0, 1)

def tokens_first(split_heads):
    return jnp.swapaxes(split_heads, 0, 1).reshape(split_heads.shape[1], -1)

def to_blocks(array_in):
    return jnp.swapaxes(array_in.reshape((array_in.shape[0], N_SEQ, TOK_DEV) + array_in.shape[2:]), 0, 1)

def segment_forward(q_raw, k_raw, v_raw, beta_logit, decay_input, log_rate, decay_bias, start_mem, bump_all):
    betas, decays = gate_values(beta_logit, decay_input, log_rate, decay_bias)
    pieces_all = (bump_all, to_blocks(q_raw), to_blocks(k_raw), to_blocks(v_raw), to_blocks(betas.T), to_blocks(decays.T))

    def one_block(memory, pieces):
        outputs, final_mem = block_forward(memory + pieces[0], pieces[1], pieces[2], pieces[3], pieces[4], pieces[5])
        return (final_mem, outputs)
    final_mem, outputs = lax.scan(one_block, start_mem, pieces_all)
    return (outputs, final_mem)

def attend(q_block, k_block, v_block, q_places, k_places):
    q_heads = q_block.reshape(q_block.shape[0], -1, AHD)
    k_heads = k_block.reshape(k_block.shape[0], -1, AHD)
    v_heads = v_block.reshape(v_block.shape[0], -1, AHD)
    scores = jnp.einsum('qhd,khd->hqk', q_heads, k_heads, precision=PRECISE) / math.sqrt(AHD)
    spread = q_places[:, None] - k_places[None, :]
    allowed = (spread >= 0) & (spread < WINDOW) & (k_places[None, :] >= 0)
    scores = jnp.where(allowed[None], scores, -1e+30)
    weights = jax.nn.softmax(scores, axis=-1)
    mixed = jnp.einsum('hqk,khd->qhd', weights, v_heads, precision=PRECISE)
    return mixed.reshape(q_block.shape[0], -1)

def window_backward(query_all, key_all, value_all, grad_all):
    row_width = query_all.shape[1]
    padding = jnp.zeros((WINDOW, row_width), jnp.float32)
    key_pad = jnp.concatenate([padding, key_all], axis=0)
    value_pad = jnp.concatenate([padding, value_all], axis=0)
    key_span = WINDOW + TOK_DEV

    def one_block(carried, block_id):
        key_acc, value_acc = carried
        start_row = (block_id * TOK_DEV).astype(jnp.int32)
        q_places = start_row + lax.iota(jnp.int32, TOK_DEV)
        k_places = start_row - WINDOW + lax.iota(jnp.int32, key_span)

        def attend_here(q_block, k_block, v_block):
            return attend(q_block, k_block, v_block, q_places, k_places)
        q_block = lax.dynamic_slice_in_dim(query_all, start_row, TOK_DEV, 0)
        k_block = lax.dynamic_slice_in_dim(key_pad, start_row, key_span, 0)
        v_block = lax.dynamic_slice_in_dim(value_pad, start_row, key_span, 0)
        primal, pullback = jax.vjp(attend_here, q_block, k_block, v_block)
        grad_q, grad_k, grad_v = pullback(lax.dynamic_slice_in_dim(grad_all, start_row, TOK_DEV, 0))
        key_acc = lax.dynamic_update_slice_in_dim(key_acc, lax.dynamic_slice_in_dim(key_acc, start_row, key_span, 0) + grad_k, start_row, 0)
        value_acc = lax.dynamic_update_slice_in_dim(value_acc, lax.dynamic_slice_in_dim(value_acc, start_row, key_span, 0) + grad_v, start_row, 0)
        return ((key_acc, value_acc), grad_q)
    (key_acc, value_acc), grad_blocks = lax.scan(one_block, (jnp.zeros_like(key_pad), jnp.zeros_like(value_pad)), jnp.arange(N_SEQ, dtype=jnp.int32))
    return (grad_blocks.reshape(TOKENS, row_width), key_acc[WINDOW:], value_acc[WINDOW:])

def reference(layer_input, beta_weight, decay_weight, log_rate, decay_bias, delta_query, delta_key, delta_value, delta_out_grad, state_init, state_grad_next, attn_query, attn_key, attn_value, attn_out_grad):
    beta_logit = jnp.dot(layer_input.astype(jnp.float32), beta_weight.T.astype(jnp.float32), preferred_element_type=jnp.float32)
    decay_input = jnp.dot(layer_input.astype(jnp.float32), decay_weight.T.astype(jnp.float32), preferred_element_type=jnp.float32)
    q_raw = heads_first(delta_query.astype(jnp.float32), HEADS)
    k_raw = heads_first(delta_key.astype(jnp.float32), HEADS)
    v_raw = heads_first(delta_value.astype(jnp.float32), HEADS)
    bump_all = jnp.zeros((N_SEQ, HEADS, DK, DV), jnp.float32)
    primal, pullback = jax.vjp(segment_forward, q_raw, k_raw, v_raw, beta_logit, decay_input, log_rate, decay_bias, state_init, bump_all)
    cotangent = (to_blocks(heads_first(delta_out_grad.astype(jnp.float32), HEADS)), state_grad_next)
    gradients = pullback(cotangent)
    grad_logit_b = gradients[3]
    grad_logit_d = gradients[4]
    input_grad = dot_high(grad_logit_b, beta_weight.astype(jnp.float32)) + dot_high(grad_logit_d, decay_weight.astype(jnp.float32))
    input_rows = layer_input.astype(jnp.float32)
    beta_weight_grad = dot_high(grad_logit_b.T, input_rows)
    decay_weight_grad = dot_high(grad_logit_d.T, input_rows)
    attn_q_grad, attn_k_grad, attn_v_grad = window_backward(attn_query.astype(jnp.float32), attn_key.astype(jnp.float32), attn_value.astype(jnp.float32), attn_out_grad.astype(jnp.float32))
    return (tokens_first(gradients[0]), tokens_first(gradients[1]), tokens_first(gradients[2]), gradients[8], input_grad, beta_weight_grad, decay_weight_grad, gradients[5], gradients[6], attn_q_grad, attn_k_grad, attn_v_grad)
```

```python
import functools
import math

import jax
import jax.numpy as jnp
from jax import lax
from jax.experimental import pallas as pl
from jax.experimental.pallas import tpu as pltpu
from jax.sharding import PartitionSpec as P

AHD = 128
WINDOW = 1024
HOP_TICKS = 3
MESH = pl.DeviceIdType.MESH
PRECISE = lax.Precision.HIGHEST
F32 = jnp.float32
BF16 = jnp.bfloat16
NN = (((1,), (0,)), ((), ()))
NT = (((1,), (1,)), ((), ()))
TN = (((0,), (0,)), ((), ()))


def parts(value):
    if isinstance(value, tuple):
        return value
    if value.dtype == BF16:
        return (value,)
    high = value.astype(BF16)
    return (high, (value - high.astype(F32)).astype(BF16))


def mul(left, right, dims=NN):
    left, right = parts(left), parts(right)
    total = None
    for i, a in reversed(list(enumerate(left))):
        for j, b in reversed(list(enumerate(right))):
            if i + j < 2:
                term = lax.dot_general(a, b, dims, preferred_element_type=F32)
                total = term if total is None else total + term
    return total


def row_sum(value):
    return jnp.sum(value, axis=1, keepdims=True)


def col_sum(value):
    return jnp.sum(value, axis=0, keepdims=True)


def grids(size):
    rows = lax.broadcasted_iota(jnp.int32, (size, size), 0)
    cols = lax.broadcasted_iota(jnp.int32, (size, size), 1)
    return rows, cols


def as_row(col, rows, cols):
    return col_sum(jnp.where(rows == cols, col, 0.0))


def head_terms(q, k, decay, rows, cols):
    kf = k.astype(F32)
    qf = q.astype(F32)
    k_norm = lax.rsqrt(row_sum(kf * kf) + 1e-06)
    q_norm = lax.rsqrt(row_sum(qf * qf) + 1e-06)
    rk = k_norm
    rq = q_norm * (1.0 / math.sqrt(q.shape[1]))
    decay_row = as_row(decay, rows, cols)
    cum = row_sum(jnp.where(cols <= rows, decay_row, 0.0))
    cum_row = as_row(cum, rows, cols)
    lower = rows >= cols
    ratios = jnp.where(lower, jnp.exp(jnp.where(lower, cum - cum_row, 0.0)), 0.0)
    growth = jnp.exp(cum)
    last = row_sum(decay_row)
    tail = jnp.exp(last - cum)
    return kf, qf, k_norm, q_norm, rk, rq, ratios, growth, jnp.exp(last), tail


def local_kernel(q_ref, k_ref, v_ref, do_ref, beta_ref, decay_ref,
                 transit_ref, offset_ref, lgrad_ref, t_ref, w_ref, uv_ref, p_ref, n_ref):
    size = q_ref.shape[0]
    count = beta_ref.shape[2]
    width = q_ref.shape[1] // count
    rows, cols = grids(size)
    inverses, systems, kept = [], [], []
    for j in range(count):
        lanes = slice(j * width, (j + 1) * width)
        q, k = q_ref[:, lanes], k_ref[:, lanes]
        beta, decay = beta_ref[0, :, j:j + 1], decay_ref[0, :, j:j + 1]
        kf, qf, _, _, rk, rq, ratios, growth, last, tail = head_terms(q, k, decay, rows, cols)
        rk_row = as_row(rk, rows, cols)
        near = jnp.where(rows > cols, ratios * (mul(k, k, NT) * rk * rk_row), 0.0)
        mixing = ratios * (mul(q, k, NT) * rq * rk_row)
        n_ref[j] = near
        p_ref[j] = mixing
        systems.append(beta * near)
        kept.append((kf * rk, qf * rq, beta, growth, last, tail, mixing))
        pair = (rows // 2 == cols // 2) & (rows > cols)
        inverses.append(jnp.where(rows == cols, 1.0, jnp.where(pair, -systems[-1], 0.0)))
    span = 2
    while span < size:
        mask = (rows // (2 * span) == cols // (2 * span)) & (rows // span > cols // span)
        split = [parts(inverse) for inverse in inverses]
        halves = [mul(split[j], jnp.where(mask, systems[j], 0.0)) for j in range(count)]
        inverses = [inverses[j] - mul(halves[j], split[j]) for j in range(count)]
        span *= 2
    for j in range(count):
        lanes = slice(j * width, (j + 1) * width)
        keys, queries, beta, growth, last, tail, mixing = kept[j]
        t_ref[j] = inverses[j]
        split = parts(inverses[j])
        w_all = mul(split, (beta * growth) * keys)
        uv_all = mul(split, beta * v_ref[:, lanes].astype(F32))
        w_ref[j] = w_all
        uv_ref[j] = uv_all
        w_split = parts(w_all)
        tail_keys = parts(keys * tail)
        transit_ref[j] = jnp.where(rows == cols, last, 0.0) - mul(tail_keys, w_split, TN)
        offset_ref[j] = mul(tail_keys, uv_all, TN)
        reach = growth * queries - mul(mixing, w_split)
        lgrad_ref[j] = mul(reach, do_ref[:, lanes], TN)


def relay_kernel(n, transit_ref, offset_ref, lgrad_ref, init_ref, next_ref, mem_ref, grad_ref,
                 send_f, recv_f, send_b, recv_b, sf_sem, rf_sem, sb_sem, rb_sem):
    me = lax.axis_index("seq")
    head = lax.axis_index("head")
    heads = transit_ref.shape[0]
    right, left = lax.rem(me + 1, n), lax.rem(me + n - 1, n)
    has_left, has_right = me > 0, me < n - 1
    barrier = pltpu.get_barrier_semaphore()

    @pl.when(has_left)
    def _():
        pl.semaphore_signal(barrier, inc=1, device_id=(left, head), device_id_type=MESH)

    @pl.when(has_right)
    def _():
        pl.semaphore_signal(barrier, inc=1, device_id=(right, head), device_id_type=MESH)

    pl.semaphore_wait(barrier, has_left.astype(jnp.int32) + has_right.astype(jnp.int32))

    def copy_f(h):
        return pltpu.make_async_remote_copy(
            src_ref=send_f.at[h], dst_ref=recv_f.at[h], send_sem=sf_sem.at[h],
            recv_sem=rf_sem.at[h], device_id=(right, head), device_id_type=MESH)

    def copy_b(h):
        return pltpu.make_async_remote_copy(
            src_ref=send_b.at[h], dst_ref=recv_b.at[h], send_sem=sb_sem.at[h],
            recv_sem=rb_sem.at[h], device_id=(left, head), device_id_type=MESH)

    def tick(t, carry):
        hf = t - HOP_TICKS * me
        hb = t - HOP_TICKS * (n - 1 - me)

        @pl.when((hf >= 0) & (hf < heads))
        def _():
            @pl.when(has_left)
            def _():
                copy_f(hf).wait_recv()
                mem_ref[hf] = recv_f[hf]

            @pl.when(jnp.logical_not(has_left))
            def _():
                mem_ref[hf] = init_ref[hf]

            @pl.when(has_right)
            def _():
                send_f[hf] = mul(transit_ref[hf], mem_ref[hf]) + offset_ref[hf]
                copy_f(hf).start()

        @pl.when((hb >= 0) & (hb < heads))
        def _():
            @pl.when(has_right)
            def _():
                copy_b(hb).wait_recv()
                grad_ref[hb] = recv_b[hb]

            @pl.when(jnp.logical_not(has_right))
            def _():
                grad_ref[hb] = next_ref[hb]

            @pl.when(has_left)
            def _():
                send_b[hb] = mul(transit_ref[hb], grad_ref[hb], TN) + lgrad_ref[hb]
                copy_b(hb).start()

        return carry

    lax.fori_loop(0, HOP_TICKS * (n - 1) + heads, tick, 0)

    def drain(h, carry):
        @pl.when(has_right)
        def _():
            copy_f(h).wait_send()

        @pl.when(has_left)
        def _():
            copy_b(h).wait_send()

        return carry

    lax.fori_loop(0, heads, drain, 0)


def grads_kernel(q_ref, k_ref, v_ref, do_ref, beta_ref, decay_ref, mem_ref, grad_ref,
                 transit_ref, lgrad_ref, t_ref, w_ref, uv_ref, p_ref, n_ref,
                 dq_ref, dk_ref, dv_ref, bound_ref, dbeta_ref, ddecay_ref):
    size = q_ref.shape[0]
    count = beta_ref.shape[2]
    width = q_ref.shape[1] // count
    rows, cols = grids(size)
    for j in range(count):
        lanes = slice(j * width, (j + 1) * width)
        q, k, do = q_ref[:, lanes], k_ref[:, lanes], do_ref[:, lanes]
        beta, decay = beta_ref[0, :, j:j + 1], decay_ref[0, :, j:j + 1]
        kf, qf, k_norm, q_norm, rk, rq, ratios, growth, last, tail = head_terms(
            q, k, decay, rows, cols)
        rk_row = as_row(rk, rows, cols)
        dof = do.astype(F32)
        memory, grad = mem_ref[j], grad_ref[j]
        near, mixing = n_ref[j], p_ref[j]
        mem_s, grad_s = parts(memory), parts(grad)
        updates = uv_ref[j] - mul(w_ref[j], mem_s)
        up_s = parts(updates)
        q_mem = rq * mul(q, mem_s)
        k_mem = rk * mul(k, mem_s)
        dup = mul(mixing, do, TN) + (rk * tail) * mul(k, grad_s)
        drhs = mul(t_ref[j], dup, TN)
        drhs_s = parts(drhs)
        dmix = jnp.where(rows >= cols, mul(do, up_s, NT), 0.0)
        dqk = dmix * ratios
        dsys = jnp.where(rows > cols, -mul(drhs_s, up_s, NT), 0.0)
        dgram = dsys * beta * ratios
        dval = beta * drhs
        dquery = growth * mul(do, mem_s, NT) + mul(dqk * rk_row, k)
        dtail = mul(up_s, grad_s, NT)
        dkey = mul(dqk * rq, q, TN) + dtail * tail
        dkey = dkey - (beta * growth) * mul(drhs_s, mem_s, NT)
        dkey = dkey + mul((dgram + dgram.T) * rk_row, k)
        dbeta = row_sum(drhs * (v_ref[:, lanes].astype(F32) - growth * k_mem))
        dbeta_ref[0, :, j:j + 1] = dbeta + row_sum(dsys * near)
        inner = dsys * (beta * near) + dmix * mixing
        tails = row_sum(dtail * kf) * (rk * tail)
        dcum = growth * (row_sum(dof * q_mem) - row_sum(dval * k_mem)) - tails + row_sum(inner)
        dcum_row = as_row(dcum, rows, cols) - col_sum(inner)
        at_end = col_sum(tails) + last * col_sum(row_sum(grad * memory))
        ddecay_ref[0, :, j:j + 1] = row_sum(jnp.where(cols >= rows, dcum_row, 0.0)) + at_end
        dq_ref[:, lanes] = rq * (dquery - qf * (q_norm * q_norm * row_sum(qf * dquery)))
        dk_ref[:, lanes] = rk * (dkey - kf * (k_norm * k_norm * row_sum(kf * dkey)))
        dv_ref[:, lanes] = dval
        bound_ref[0, j] = mul(transit_ref[j], grad_s, TN) + lgrad_ref[j]


def attn_rows_kernel(start_ref, q_ref, g_ref, k_ref, v_ref, dq_ref, stat_ref):
    size = q_ref.shape[0]
    span = k_ref.shape[0] * k_ref.shape[1]
    scale = 1.0 / math.sqrt(AHD)
    keys = k_ref[...].reshape(span, AHD)
    values = v_ref[...].reshape(span, AHD)
    gap = (start_ref[0] + lax.broadcasted_iota(jnp.int32, (size, span), 0)
           - lax.broadcasted_iota(jnp.int32, (size, span), 1))
    scores = mul(q_ref[...], keys, NT) * scale
    scores = jnp.where((gap >= 0) & (gap < WINDOW), scores, -1e30)
    top = jnp.max(scores, axis=1, keepdims=True)
    weights = jnp.exp(scores - top)
    inverse = 1.0 / row_sum(weights)
    weights = weights * inverse
    weight_grad = mul(g_ref[...], values, NT)
    row_term = row_sum(weights * weight_grad)
    dscores = weights * (weight_grad - row_term) * scale
    dq_ref[...] = mul(dscores, keys)
    stat_ref[0, :, 0:1] = top
    stat_ref[0, :, 1:2] = inverse
    stat_ref[0, :, 2:3] = row_term


def attn_keys_kernel(start_ref, k_ref, v_ref, q_ref, g_ref, stat_ref, dk_ref, dv_ref):
    size = k_ref.shape[0]
    span = q_ref.shape[0] * q_ref.shape[1]
    scale = 1.0 / math.sqrt(AHD)
    queries = q_ref[...].reshape(span, AHD)
    grads = g_ref[...].reshape(span, AHD)
    stats = stat_ref[...].reshape(span, stat_ref.shape[3])
    gap = (start_ref[0] + lax.broadcasted_iota(jnp.int32, (span, size), 0)
           - lax.broadcasted_iota(jnp.int32, (span, size), 1))
    allowed = (gap >= 0) & (gap < WINDOW)
    scores = mul(queries, k_ref[...], NT) * scale
    weights = jnp.where(allowed, jnp.exp(jnp.where(allowed, scores - stats[:, 0:1], 0.0)), 0.0)
    weights = weights * stats[:, 1:2]
    weight_grad = mul(grads, v_ref[...], NT)
    dscores = weights * (weight_grad - stats[:, 2:3]) * scale
    dv_ref[...] = mul(weights, grads, TN)
    dk_ref[...] = mul(dscores, queries, TN)


def attention(attn_query, attn_key, attn_value, attn_out_grad, n, me):
    size, width = attn_query.shape
    heads = width // AHD
    reach = min(-(-WINDOW // size), n - 1)
    span = reach + 1
    gathered = lax.all_gather(
        jnp.concatenate([attn_query, attn_key, attn_value, attn_out_grad], axis=1), "seq")
    first = jnp.clip(me - reach, 0, n - span)
    after = jnp.clip(me, 0, n - span)
    earlier = later = gathered
    if span < n:
        earlier = lax.dynamic_slice_in_dim(gathered, first, span, 0)
        later = lax.dynamic_slice_in_dim(gathered, after, span, 0)

    def own():
        return pl.BlockSpec((size, AHD), lambda h: (0, h))

    def others(group):
        return pl.BlockSpec((span, size, AHD), lambda h: (0, 0, group * heads + h))

    smem = pl.BlockSpec(memory_space=pltpu.SMEM)
    wide = jax.ShapeDtypeStruct((size, width), F32)
    params = pltpu.CompilerParams(vmem_limit_bytes=40 * 1024 * 1024)
    cost = pl.CostEstimate(flops=6 * size * span * size * width, bytes_accessed=8 * span * size * width, transcendentals=size * span * size * heads)
    dquery, stats = pl.pallas_call(
        attn_rows_kernel,
        grid=(heads,),
        out_shape=(wide, jax.ShapeDtypeStruct((heads, size, 3), F32)),
        in_specs=[smem, own(), own(), others(1), others(2)],
        out_specs=(own(), pl.BlockSpec((1, size, 3), lambda h: (h, 0, 0))),
        compiler_params=params, cost_estimate=cost, name="attn_rows",
    )(((me - first) * size).reshape(1).astype(jnp.int32), attn_query, attn_out_grad, earlier, earlier)
    every = lax.all_gather(stats, "seq")
    if span < n:
        every = lax.dynamic_slice_in_dim(every, after, span, 0)
    dkey, dvalue = pl.pallas_call(
        attn_keys_kernel,
        grid=(heads,),
        out_shape=(wide, wide),
        in_specs=[smem, own(), own(), others(0), others(3),
                  pl.BlockSpec((span, 1, size, 3), lambda h: (0, h, 0, 0))],
        out_specs=(own(), own()),
        compiler_params=params, cost_estimate=cost, name="attn_keys",
    )(((after - me) * size).reshape(1).astype(jnp.int32), attn_key, attn_value, later, later, every)
    return dquery, dkey, dvalue


def delta(delta_query, delta_key, delta_value, delta_out_grad, betas, decays,
          state_init, state_grad_next, n):
    size, width = delta_query.shape
    heads = betas.shape[1]
    dim = width // heads
    group = next(c for c in (4, 2, 1) if heads % c == 0)
    steps = heads // group

    def by_step(flat):
        return jnp.swapaxes(flat.reshape(size, steps, group), 0, 1)

    tokens = pl.BlockSpec((size, group * dim), lambda i: (0, i))
    gate = pl.BlockSpec((1, size, group), lambda i: (i, 0, 0))
    square = pl.BlockSpec((group, dim, dim), lambda i: (i, 0, 0))
    pairs = pl.BlockSpec((group, size, size), lambda i: (i, 0, 0))
    token_rows = pl.BlockSpec((group, size, dim), lambda i: (i, 0, 0))
    state = jax.ShapeDtypeStruct((heads, dim, dim), F32)
    pair = jax.ShapeDtypeStruct((heads, size, size), F32)
    per_token = jax.ShapeDtypeStruct((heads, size, dim), F32)
    params = pltpu.CompilerParams(vmem_limit_bytes=48 * 1024 * 1024)
    beta_steps, decay_steps = by_step(betas), by_step(decays)
    flops = 2 * heads * size * size * dim
    transit, offset, lgrad, inverse, w_all, uv_all, mixing, near = pl.pallas_call(
        local_kernel,
        grid=(steps,),
        out_shape=(state, state, state, pair, per_token, per_token, pair, pair),
        in_specs=[tokens] * 4 + [gate] * 2,
        out_specs=(square, square, square, pairs, token_rows, token_rows, pairs, pairs),
        compiler_params=params, name="delta_local",
        cost_estimate=pl.CostEstimate(flops=60 * flops, bytes_accessed=6 << 20, transcendentals=0),
    )(delta_query, delta_key, delta_value, delta_out_grad, beta_steps, decay_steps)
    vmem = pl.BlockSpec(memory_space=pltpu.VMEM)
    sem = pltpu.SemaphoreType.DMA((heads,))
    box = pltpu.VMEM((heads, dim, dim), F32)
    mem_in, grad_end = pl.pallas_call(
        functools.partial(relay_kernel, n),
        out_shape=(state, state),
        in_specs=[vmem] * 5,
        out_specs=(vmem, vmem),
        scratch_shapes=[box, box, box, box, sem, sem, sem, sem],
        compiler_params=pltpu.CompilerParams(
            collective_id=0, has_side_effects=True, vmem_limit_bytes=32 * 1024 * 1024),
        name="state_relay",
        cost_estimate=pl.CostEstimate(flops=6 * flops, bytes_accessed=4 << 20, transcendentals=0),
    )(transit, offset, lgrad, state_init, state_grad_next)
    flat = jax.ShapeDtypeStruct((size, width), F32)
    gate_out = jax.ShapeDtypeStruct((steps, size, group), F32)
    dq, dk, dv, boundary, dbeta, ddecay = pl.pallas_call(
        grads_kernel,
        grid=(steps,),
        out_shape=(flat, flat, flat, jax.ShapeDtypeStruct((1, heads, dim, dim), F32),
                   gate_out, gate_out),
        in_specs=[tokens] * 4 + [gate] * 2 + [square] * 4 + [pairs, token_rows, token_rows, pairs, pairs],
        out_specs=(tokens, tokens, tokens,
                   pl.BlockSpec((1, group, dim, dim), lambda i: (0, i, 0, 0)), gate, gate),
        compiler_params=params, name="delta_grads",
        cost_estimate=pl.CostEstimate(flops=50 * flops, bytes_accessed=9 << 20, transcendentals=0),
    )(delta_query, delta_key, delta_value, delta_out_grad, beta_steps, decay_steps,
      mem_in, grad_end, transit, lgrad, inverse, w_all, uv_all, mixing, near)

    def by_token(stepped):
        return jnp.swapaxes(stepped, 0, 1).reshape(size, heads)

    return dq, dk, dv, boundary, by_token(dbeta), by_token(ddecay)


def dot_high(left_mat, right_mat):
    return jnp.matmul(left_mat, right_mat, precision=PRECISE)


def gate_values(beta_logit, decay_input, log_rate, decay_bias):
    betas = jax.nn.sigmoid(beta_logit)
    decays = -jnp.exp(log_rate)[None, :] * jax.nn.softplus(decay_input + decay_bias[None, :])
    return (betas, decays)


def shards(layer_input, beta_weight, decay_weight, log_rate, decay_bias, delta_query, delta_key,
           delta_value, delta_out_grad, state_init, state_grad_next, attn_query, attn_key,
           attn_value, attn_out_grad):
    n = lax.axis_size("seq")
    me = lax.axis_index("seq")
    heads = beta_weight.shape[0]
    both_weight = jnp.concatenate([beta_weight, decay_weight], axis=0)
    logits = lax.dot_general(layer_input, both_weight, NT, preferred_element_type=F32)
    (betas, decays), pull_gate = jax.vjp(
        gate_values, logits[:, :heads], logits[:, heads:], log_rate, decay_bias)
    cols = lax.all_to_all(both_weight, "head", split_axis=1, concat_axis=0, tiled=True)
    dquery, dkey, dvalue = attention(attn_query, attn_key, attn_value, attn_out_grad, n, me)
    dq, dk, dv, boundary, dbeta, ddecay = delta(
        delta_query, delta_key, delta_value, delta_out_grad, betas, decays,
        state_init, state_grad_next, n)
    grad_b, grad_d, grad_rate, grad_bias = pull_gate((dbeta, ddecay))
    mine = jnp.concatenate([grad_b, grad_d], axis=1)
    every = lax.all_gather(mine, "head", axis=1, tiled=True)
    input_grad = dot_high(every, cols.astype(F32))
    terms = dot_high(mine.T, layer_input.astype(F32))
    weight_grad = lax.psum_scatter(terms, "seq", scatter_dimension=1, tiled=True)
    params = lax.psum(jnp.stack([grad_rate, grad_bias]), "seq")
    return (dq, dk, dv, boundary, input_grad, weight_grad[:heads], weight_grad[heads:],
            params[0], params[1], dquery, dkey, dvalue)


def solution(mesh):
    rows, heads, both = P("seq", None), P("head"), P("seq", "head")
    wide, state = P("head", None), P("head", None, None)
    return jax.shard_map(
        shards,
        mesh=mesh,
        in_specs=(rows, wide, wide, heads, heads, both, both, both, both, state, state,
                  both, both, both, both),
        out_specs=(both, both, both, P("seq", "head", None, None), both, P("head", "seq"),
                   P("head", "seq"), heads, heads, both, both, both),
        check_vma=False,
    )
```

```python
import functools
import math

import jax
import jax.numpy as jnp
from jax import lax
from jax.experimental import pallas as pl
from jax.experimental.pallas import tpu as pltpu
from jax.sharding import PartitionSpec as P

AHD = 128
WINDOW = 1024
HOP_TICKS = 3
MESH = pl.DeviceIdType.MESH
F32 = jnp.float32
BF16 = jnp.bfloat16
NN = (((1,), (0,)), ((), ()))
NT = (((1,), (1,)), ((), ()))
TN = (((0,), (0,)), ((), ()))


def parts(value):
    if isinstance(value, tuple):
        return value
    if value.dtype == BF16:
        return (value,)
    high = value.astype(BF16)
    return (high, (value - high.astype(F32)).astype(BF16))


def mul(left, right, dims=NN):
    left, right = parts(left), parts(right)
    total = None
    for i, a in reversed(list(enumerate(left))):
        for j, b in reversed(list(enumerate(right))):
            if i + j < 2:
                term = lax.dot_general(a, b, dims, preferred_element_type=F32)
                total = term if total is None else total + term
    return total


def row_sum(value):
    return jnp.sum(value, axis=1, keepdims=True)


def col_sum(value):
    return jnp.sum(value, axis=0, keepdims=True)


def grids(size):
    rows = lax.broadcasted_iota(jnp.int32, (size, size), 0)
    cols = lax.broadcasted_iota(jnp.int32, (size, size), 1)
    return rows, cols


def as_row(col, rows, cols):
    return col_sum(jnp.where(rows == cols, col, 0.0))


def as_col(row, rows, cols):
    return row_sum(jnp.where(rows == cols, row, 0.0))


def head_terms(q, k, decay_row, rows, cols):
    kf = k.astype(F32)
    qf = q.astype(F32)
    k_norm = lax.rsqrt(row_sum(kf * kf) + 1e-06)
    q_norm = lax.rsqrt(row_sum(qf * qf) + 1e-06)
    rk = k_norm
    rq = q_norm * (1.0 / math.sqrt(q.shape[1]))
    cum = row_sum(jnp.where(cols <= rows, decay_row, 0.0))
    cum_row = as_row(cum, rows, cols)
    lower = rows >= cols
    ratios = jnp.where(lower, jnp.exp(jnp.where(lower, cum - cum_row, 0.0)), 0.0)
    growth = jnp.exp(cum)
    last = row_sum(decay_row)
    tail = jnp.exp(last - cum)
    return kf, qf, k_norm, q_norm, rk, rq, ratios, growth, jnp.exp(last), tail


def local_kernel(q_ref, k_ref, v_ref, do_ref, beta_ref, decay_ref,
                 transit_ref, offset_ref, lgrad_ref, t_ref, w_ref, uv_ref, p_ref, n_ref):
    size = q_ref.shape[0]
    count = beta_ref.shape[1]
    width = q_ref.shape[1] // count
    rows, cols = grids(size)
    inverses, systems, kept = [], [], []
    for j in range(count):
        lanes = slice(j * width, (j + 1) * width)
        q, k = q_ref[:, lanes], k_ref[:, lanes]
        beta, decay = as_col(beta_ref[0, j:j + 1, :], rows, cols), decay_ref[0, j:j + 1, :]
        kf, qf, _, _, rk, rq, ratios, growth, last, tail = head_terms(q, k, decay, rows, cols)
        rk_row = as_row(rk, rows, cols)
        near = jnp.where(rows > cols, ratios * (mul(k, k, NT) * rk * rk_row), 0.0)
        mixing = ratios * (mul(q, k, NT) * rq * rk_row)
        n_ref[j] = near
        p_ref[j] = mixing
        systems.append(beta * near)
        kept.append((kf * rk, qf * rq, beta, growth, last, tail, mixing))
        pair = (rows // 2 == cols // 2) & (rows > cols)
        inverses.append(jnp.where(rows == cols, 1.0, jnp.where(pair, -systems[-1], 0.0)))
    span = 2
    while span < size:
        mask = (rows // (2 * span) == cols // (2 * span)) & (rows // span > cols // span)
        split = [parts(inverse) for inverse in inverses]
        halves = [mul(split[j], jnp.where(mask, systems[j], 0.0)) for j in range(count)]
        inverses = [inverses[j] - mul(halves[j], split[j]) for j in range(count)]
        span *= 2
    for j in range(count):
        lanes = slice(j * width, (j + 1) * width)
        keys, queries, beta, growth, last, tail, mixing = kept[j]
        t_ref[j] = inverses[j]
        split = parts(inverses[j])
        w_all = mul(split, (beta * growth) * keys)
        uv_all = mul(split, beta * v_ref[:, lanes].astype(F32))
        w_ref[j] = w_all
        uv_ref[j] = uv_all
        w_split = parts(w_all)
        tail_keys = parts(keys * tail)
        transit_ref[j] = jnp.where(rows == cols, last, 0.0) - mul(tail_keys, w_split, TN)
        offset_ref[j] = mul(tail_keys, uv_all, TN)
        reach = growth * queries - mul(mixing, w_split)
        lgrad_ref[j] = mul(reach, do_ref[:, lanes], TN)


def meet(n, m, me, head):
    barrier = pltpu.get_barrier_semaphore()
    for d in range(1, n):
        pl.semaphore_signal(barrier, inc=1, device_id=(lax.rem(me + d, n), head),
                            device_id_type=MESH)
    for d in range(1, m):
        pl.semaphore_signal(barrier, inc=1, device_id=(me, lax.rem(head + d, m)),
                            device_id_type=MESH)
    return lambda: pl.semaphore_wait(barrier, n + m - 2)


def remote(src, dst, send, recv, device):
    return pltpu.make_async_remote_copy(src_ref=src, dst_ref=dst, send_sem=send, recv_sem=recv,
                                        device_id=device, device_id_type=MESH)


def relay_kernel(n, m, span, q_ref, k_ref, v_ref, do_ref, beta_ref, decay_ref, init_ref, next_ref,
                 bw_ref, dw_ref, aq_ref, ak_ref, av_ref, ag_ref,
                 transit_ref, lgrad_ref, t_ref, w_ref, uv_ref, p_ref, n_ref, mem_ref, grad_ref,
                 weight_ref, kv_ref, qg_ref,
                 offset_ref, slices, send_f, recv_f, send_b, recv_b, sf_sem, rf_sem, sb_sem, rb_sem,
                 skv_sem, rkv_sem, sqg_sem, rqg_sem, sw_sem, rw_sem):
    me = lax.axis_index("seq")
    head = lax.axis_index("head")
    heads = init_ref.shape[0]
    steps, group, _ = beta_ref.shape
    right, left = lax.rem(me + 1, n), lax.rem(me + n - 1, n)
    has_left, has_right = me > 0, me < n - 1
    entered = meet(n, m, me, head)
    width = ak_ref.shape[1]
    kv_ref[0, :, :width] = ak_ref[...]
    kv_ref[0, :, width:] = av_ref[...]
    qg_ref[0, :, :width] = aq_ref[...]
    qg_ref[0, :, width:] = ag_ref[...]
    part = bw_ref.shape[1] // m
    for p in range(m):
        lanes = slice(p * part, (p + 1) * part)
        slices[p, :heads] = bw_ref[:, lanes].astype(F32)
        slices[p, heads:] = dw_ref[:, lanes].astype(F32)
    weight_ref[head] = slices[head]
    entered()

    def copy_kv(d):
        return remote(kv_ref.at[0], kv_ref.at[d], skv_sem.at[d], rkv_sem.at[d],
                      (lax.rem(me + d, n), head))

    def copy_qg(d):
        return remote(qg_ref.at[0], qg_ref.at[d], sqg_sem.at[d], rqg_sem.at[d],
                      (lax.rem(me + n - d, n), head))

    def copy_weight(d):
        peer = lax.rem(head + d, m)
        return remote(slices.at[peer], weight_ref.at[head], sw_sem.at[d], rw_sem.at[d], (me, peer))

    def came_weight(d):
        peer = lax.rem(head + m - d, m)
        return remote(slices.at[peer], weight_ref.at[peer], sw_sem.at[d], rw_sem.at[d], (me, peer))

    for d in range(1, m):
        copy_weight(d).start()
    for d in range(1, span):
        @pl.when(me + d < n)
        def _(d=d):
            copy_kv(d).start()

        @pl.when(me >= d)
        def _(d=d):
            copy_qg(d).start()

        @pl.when(me < d)
        def _(d=d):
            kv_ref[d] = jnp.zeros(kv_ref.shape[1:], BF16)

        @pl.when(me + d >= n)
        def _(d=d):
            qg_ref[d] = jnp.zeros(qg_ref.shape[1:], BF16)

    lane_count = q_ref.shape[1] // steps

    def local_step(i, carry):
        lanes = pl.ds(pl.multiple_of(i * lane_count, 128), lane_count)
        mine = pl.ds(i * group, group)
        local_kernel(q_ref.at[:, lanes], k_ref.at[:, lanes], v_ref.at[:, lanes],
                     do_ref.at[:, lanes], beta_ref.at[pl.ds(i, 1)], decay_ref.at[pl.ds(i, 1)],
                     transit_ref.at[mine], offset_ref.at[mine], lgrad_ref.at[mine], t_ref.at[mine],
                     w_ref.at[mine], uv_ref.at[mine], p_ref.at[mine], n_ref.at[mine])
        return carry

    lax.fori_loop(0, steps, local_step, 0)

    def copy_f(h):
        return pltpu.make_async_remote_copy(
            src_ref=send_f.at[h], dst_ref=recv_f.at[h], send_sem=sf_sem.at[h],
            recv_sem=rf_sem.at[h], device_id=(right, head), device_id_type=MESH)

    def copy_b(h):
        return pltpu.make_async_remote_copy(
            src_ref=send_b.at[h], dst_ref=recv_b.at[h], send_sem=sb_sem.at[h],
            recv_sem=rb_sem.at[h], device_id=(left, head), device_id_type=MESH)

    def tick(t, carry):
        hf = t - HOP_TICKS * me
        hb = t - HOP_TICKS * (n - 1 - me)

        @pl.when((hf >= 0) & (hf < heads))
        def _():
            @pl.when(has_left)
            def _():
                copy_f(hf).wait_recv()
                mem_ref[hf] = recv_f[hf]

            @pl.when(jnp.logical_not(has_left))
            def _():
                mem_ref[hf] = init_ref[hf]

            @pl.when(has_right)
            def _():
                send_f[hf] = mul(transit_ref[hf], mem_ref[hf]) + offset_ref[hf]
                copy_f(hf).start()

        @pl.when((hb >= 0) & (hb < heads))
        def _():
            @pl.when(has_right)
            def _():
                copy_b(hb).wait_recv()
                grad_ref[hb] = recv_b[hb]

            @pl.when(jnp.logical_not(has_right))
            def _():
                grad_ref[hb] = next_ref[hb]

            @pl.when(has_left)
            def _():
                send_b[hb] = mul(transit_ref[hb], grad_ref[hb], TN) + lgrad_ref[hb]
                copy_b(hb).start()

        return carry

    lax.fori_loop(0, HOP_TICKS * (n - 1) + heads, tick, 0)

    def drain(h, carry):
        @pl.when(has_right)
        def _():
            copy_f(h).wait_send()

        @pl.when(has_left)
        def _():
            copy_b(h).wait_send()

        return carry

    lax.fori_loop(0, heads, drain, 0)
    for d in range(1, m):
        came_weight(d).wait_recv()
        copy_weight(d).wait_send()
    for d in range(1, span):
        @pl.when(me + d < n)
        def _(d=d):
            copy_kv(d).wait_send()
            copy_qg(d).wait_recv()

        @pl.when(me >= d)
        def _(d=d):
            copy_qg(d).wait_send()
            copy_kv(d).wait_recv()


def grads_kernel(q_ref, k_ref, v_ref, do_ref, beta_ref, decay_ref, mem_ref, grad_ref,
                 transit_ref, lgrad_ref, t_ref, w_ref, uv_ref, p_ref, n_ref,
                 dq_ref, dk_ref, dv_ref, bound_ref, dbeta_ref, ddecay_ref):
    size = q_ref.shape[0]
    count = beta_ref.shape[1]
    width = q_ref.shape[1] // count
    rows, cols = grids(size)
    for j in range(count):
        lanes = slice(j * width, (j + 1) * width)
        q, k, do = q_ref[:, lanes], k_ref[:, lanes], do_ref[:, lanes]
        beta, decay = as_col(beta_ref[0, j:j + 1, :], rows, cols), decay_ref[0, j:j + 1, :]
        kf, qf, k_norm, q_norm, rk, rq, ratios, growth, last, tail = head_terms(
            q, k, decay, rows, cols)
        rk_row = as_row(rk, rows, cols)
        dof = do.astype(F32)
        memory, grad = mem_ref[j], grad_ref[j]
        near, mixing = n_ref[j], p_ref[j]
        mem_s, grad_s = parts(memory), parts(grad)
        updates = uv_ref[j] - mul(w_ref[j], mem_s)
        up_s = parts(updates)
        q_mem = rq * mul(q, mem_s)
        k_mem = rk * mul(k, mem_s)
        dup = mul(mixing, do, TN) + (rk * tail) * mul(k, grad_s)
        drhs = mul(t_ref[j], dup, TN)
        drhs_s = parts(drhs)
        dmix = jnp.where(rows >= cols, mul(do, up_s, NT), 0.0)
        dqk = dmix * ratios
        dsys = jnp.where(rows > cols, -mul(drhs_s, up_s, NT), 0.0)
        dgram = dsys * beta * ratios
        dval = beta * drhs
        dquery = growth * mul(do, mem_s, NT) + mul(dqk * rk_row, k)
        dtail = mul(up_s, grad_s, NT)
        dkey = mul(dqk * rq, q, TN) + dtail * tail
        dkey = dkey - (beta * growth) * mul(drhs_s, mem_s, NT)
        dkey = dkey + mul((dgram + dgram.T) * rk_row, k)
        dbeta = row_sum(drhs * (v_ref[:, lanes].astype(F32) - growth * k_mem))
        dbeta_ref[0, j:j + 1, :] = as_row(dbeta + row_sum(dsys * near), rows, cols)
        inner = dsys * (beta * near) + dmix * mixing
        tails = row_sum(dtail * kf) * (rk * tail)
        dcum = growth * (row_sum(dof * q_mem) - row_sum(dval * k_mem)) - tails + row_sum(inner)
        dcum_row = as_row(dcum, rows, cols) - col_sum(inner)
        at_end = col_sum(tails) + last * col_sum(row_sum(grad * memory))
        after = row_sum(jnp.where(cols >= rows, dcum_row, 0.0)) + at_end
        ddecay_ref[0, j:j + 1, :] = as_row(after, rows, cols)
        dq_ref[:, lanes] = rq * (dquery - qf * (q_norm * q_norm * row_sum(qf * dquery)))
        dk_ref[:, lanes] = rk * (dkey - kf * (k_norm * k_norm * row_sum(kf * dkey)))
        dv_ref[:, lanes] = dval
        bound_ref[0, j] = mul(transit_ref[j], grad_s, TN) + lgrad_ref[j]


def attn_rows_kernel(place_ref, q_ref, g_ref, k_ref, v_ref, dq_ref, stat_ref):
    size = q_ref.shape[0]
    count = k_ref.shape[0]
    span = count * size
    scale = 1.0 / math.sqrt(AHD)
    keys = k_ref[...].reshape(span, AHD)
    values = v_ref[...].reshape(span, AHD)
    rows = lax.broadcasted_iota(jnp.int32, (size, span), 0)
    cols = lax.broadcasted_iota(jnp.int32, (size, span), 1)
    back = cols // size
    gap = rows - cols % size + back * size
    allowed = (gap >= 0) & (gap < WINDOW) & (back <= place_ref[0])
    scores = jnp.where(allowed, mul(q_ref[...], keys, NT) * scale, -1e30)
    top = jnp.max(scores, axis=1, keepdims=True)
    weights = jnp.exp(scores - top)
    inverse = 1.0 / row_sum(weights)
    weights = weights * inverse
    weight_grad = mul(g_ref[...], values, NT)
    row_term = row_sum(weights * weight_grad)
    dscores = weights * (weight_grad - row_term) * scale
    dq_ref[...] = mul(dscores, keys)
    square = grids(size)
    stat_ref[0] = jnp.zeros(stat_ref.shape[1:], F32)
    stat_ref[0, 0:1, :] = as_row(top, *square)
    stat_ref[0, 1:2, :] = as_row(inverse, *square)
    stat_ref[0, 2:3, :] = as_row(row_term, *square)


def tail_kernel(n, m, span, x_ref, dbeta_ref, ddecay_ref, beta_ref, decay_ref, slope_ref,
                weight_ref, ak_ref, av_ref, qg_ref, stat_ref,
                input_ref, wsum_ref, dk_ref, dv_ref,
                terms, arrived, every, stats, st_sem, rt_sem, se_sem, re_sem, ss_sem, rs_sem):
    me = lax.axis_index("seq")
    head = lax.axis_index("head")
    entered = meet(n, m, me, head)
    heads, size = beta_ref.shape
    part = x_ref.shape[1] // n
    betas, ddecay = beta_ref[...], ddecay_ref[...]
    grad_d = ddecay * slope_ref[...]
    every[head, :heads] = dbeta_ref[...] * (betas * (1.0 - betas))
    every[head, heads:] = grad_d
    stats[0] = stat_ref[...]
    lane = lax.broadcasted_iota(jnp.int32, (heads, size), 1)
    params = jnp.where(lane == 0, row_sum(ddecay * decay_ref[...]),
                       jnp.where(lane == 1, row_sum(grad_d), 0.0))
    mine = parts(every[head])
    entered()

    def copy_stat(d):
        return remote(stats.at[0], stats.at[d], ss_sem.at[d], rs_sem.at[d],
                      (lax.rem(me + n - d, n), head))

    def copy_every(d):
        return remote(every.at[head], every.at[head], se_sem.at[d], re_sem.at[d],
                      (me, lax.rem(head + d, m)))

    def came_every(d):
        peer = lax.rem(head + m - d, m)
        return remote(every.at[peer], every.at[peer], se_sem.at[d], re_sem.at[d], (me, peer))

    def copy_term(d):
        return remote(terms.at[d], arrived.at[d], st_sem.at[d], rt_sem.at[d],
                      (lax.rem(me + d, n), head))

    for d in range(1, span):
        @pl.when(me >= d)
        def _(d=d):
            copy_stat(d).start()

        @pl.when(me + d >= n)
        def _(d=d):
            stats[d] = jnp.zeros(stats.shape[1:], F32)
    for d in range(1, m):
        copy_every(d).start()

    def fill(d):
        place = pl.multiple_of(lax.rem(me + d, n) * part, 128)
        terms[d] = jnp.zeros(terms.shape[1:], F32)
        terms[d, :2 * heads] = mul(mine, x_ref[:, pl.ds(place, part)])
        terms[d, 2 * heads:, :size] = params

    def send_term(d, carry):
        fill(d)
        copy_term(d).start()
        return carry

    lax.fori_loop(1, n, send_term, 0)
    fill(0)
    for d in range(1, span):
        @pl.when(me + d < n)
        def _(d=d):
            copy_stat(d).wait_recv()
    scale = 1.0 / math.sqrt(AHD)
    rows, cols = grids(size)
    width = ak_ref.shape[1]
    for h in range(width // AHD):
        lanes = slice(h * AHD, (h + 1) * AHD)
        more = slice(width + h * AHD, width + (h + 1) * AHD)
        key, value = ak_ref[:, lanes], av_ref[:, lanes]
        dkey = dvalue = jnp.zeros((size, AHD), F32)
        for d in range(span):
            query, grad = qg_ref[d, :, lanes], qg_ref[d, :, more]
            gap = cols - rows + d * size
            allowed = (gap >= 0) & (gap < WINDOW)
            scores = mul(key, query, NT) * scale - stats[d, h, 0:1, :]
            weights = jnp.where(allowed, jnp.exp(jnp.where(allowed, scores, 0.0)), 0.0)
            weights = weights * stats[d, h, 1:2, :]
            dscores = weights * (mul(value, grad, NT) - stats[d, h, 2:3, :]) * scale
            dvalue = dvalue + mul(weights, grad)
            dkey = dkey + mul(dscores, query)
        dk_ref[:, lanes] = dkey
        dv_ref[:, lanes] = dvalue
    for d in range(1, m):
        came_every(d).wait_recv()
    left = parts(every[...].reshape(m * 2 * heads, size))
    chunk = next(c for c in (512, 256, 128) if weight_ref.shape[2] % c == 0)
    for c in range(0, weight_ref.shape[2], chunk):
        right = weight_ref[:, :, c:c + chunk].reshape(m * 2 * heads, chunk).astype(BF16)
        input_ref[:, c:c + chunk] = mul(left, right, TN)
    total = terms[0]
    for d in range(1, n):
        copy_term(d).wait_recv()
        total = total + arrived[d]
    wsum_ref[...] = total
    for d in range(1, span):
        @pl.when(me >= d)
        def _(d=d):
            copy_stat(d).wait_send()
    for d in range(1, m):
        copy_every(d).wait_send()
    for d in range(1, n):
        copy_term(d).wait_send()


def shards(layer_input, beta_weight, decay_weight, log_rate, decay_bias, delta_query, delta_key,
           delta_value, delta_out_grad, state_init, state_grad_next, attn_query, attn_key,
           attn_value, attn_out_grad):
    n, m = lax.axis_size("seq"), lax.axis_size("head")
    me = lax.axis_index("seq")
    size, width = delta_query.shape
    heads = beta_weight.shape[0]
    features = layer_input.shape[1]
    dim = width // heads
    group = next(c for c in (4, 2, 1) if heads % c == 0)
    steps = heads // group
    attn_width = attn_query.shape[1]
    attn_heads = attn_width // AHD
    span = min(-(-WINDOW // size), n - 1) + 1

    betas = jax.nn.sigmoid(lax.dot_general(beta_weight, layer_input, NT, preferred_element_type=F32))
    shifted = lax.dot_general(decay_weight, layer_input, NT, preferred_element_type=F32)
    shifted = shifted + decay_bias[:, None]
    rate = -jnp.exp(log_rate)[:, None]
    decays = rate * jax.nn.softplus(shifted)
    slope = rate * jax.nn.sigmoid(shifted)

    def shape(*dims, kind=F32):
        return jax.ShapeDtypeStruct(dims, kind)

    def params(mib, **more):
        return pltpu.CompilerParams(vmem_limit_bytes=mib * 1024 * 1024, **more)

    def cost(flops, mib):
        return pl.CostEstimate(flops=flops, bytes_accessed=mib << 20, transcendentals=0)

    vmem = pl.BlockSpec(memory_space=pltpu.VMEM)
    state, pair = shape(heads, dim, dim), shape(heads, size, size)
    per_token = shape(heads, size, dim)
    box, sem = pltpu.VMEM((heads, dim, dim), F32), pltpu.SemaphoreType.DMA
    beta_steps = betas.reshape(steps, group, size)
    decay_steps = decays.reshape(steps, group, size)
    flops = 2 * heads * size * size * dim
    (transit, lgrad, inverse, w_all, uv_all, mixing, near, mem_in, grad_end, weight_cols, kv_all,
     qg_all) = pl.pallas_call(
        functools.partial(relay_kernel, n, m, span),
        out_shape=(state, state, pair, per_token, per_token, pair, pair, state, state,
                   shape(m, 2 * heads, features // m),
                   shape(span, size, 2 * attn_width, kind=BF16),
                   shape(span, size, 2 * attn_width, kind=BF16)),
        in_specs=[vmem] * 14,
        out_specs=(vmem,) * 12,
        scratch_shapes=[box, pltpu.VMEM((m, 2 * heads, features // m), F32), box, box, box, box,
                        sem((heads,)), sem((heads,)), sem((heads,)), sem((heads,)),
                        sem((span,)), sem((span,)), sem((span,)), sem((span,)), sem((m,)), sem((m,))],
        compiler_params=params(48, collective_id=0, has_side_effects=True),
        name="state_relay", cost_estimate=cost(66 * flops, 16),
    )(delta_query, delta_key, delta_value, delta_out_grad, beta_steps, decay_steps, state_init,
      state_grad_next, beta_weight, decay_weight, attn_query, attn_key, attn_value, attn_out_grad)

    def own():
        return pl.BlockSpec((size, AHD), lambda h: (0, h))

    def others(part):
        return pl.BlockSpec((span, size, AHD), lambda h: (0, 0, part * attn_heads + h))

    attn_flops = 2 * size * span * size * attn_width
    dquery, stats = pl.pallas_call(
        attn_rows_kernel,
        grid=(attn_heads,),
        out_shape=(shape(size, attn_width), shape(attn_heads, 8, size)),
        in_specs=[pl.BlockSpec(memory_space=pltpu.SMEM), own(), own(), others(0), others(1)],
        out_specs=(own(), pl.BlockSpec((1, 8, size), lambda h: (h, 0, 0))),
        compiler_params=params(40), cost_estimate=cost(4 * attn_flops, 3), name="attn_rows",
    )(me.reshape(1).astype(jnp.int32), attn_query, attn_out_grad, kv_all, kv_all)

    tokens = pl.BlockSpec((size, group * dim), lambda i: (0, i))
    gate = pl.BlockSpec((1, group, size), lambda i: (i, 0, 0))
    square = pl.BlockSpec((group, dim, dim), lambda i: (i, 0, 0))
    pairs = pl.BlockSpec((group, size, size), lambda i: (i, 0, 0))
    token_rows = pl.BlockSpec((group, size, dim), lambda i: (i, 0, 0))
    flat, gate_out = shape(size, width), shape(steps, group, size)
    dq, dk, dv, boundary, dbeta, ddecay = pl.pallas_call(
        grads_kernel,
        grid=(steps,),
        out_shape=(flat, flat, flat, shape(1, heads, dim, dim), gate_out, gate_out),
        in_specs=[tokens] * 4 + [gate] * 2 + [square] * 4 + [pairs, token_rows, token_rows, pairs, pairs],
        out_specs=(tokens, tokens, tokens,
                   pl.BlockSpec((1, group, dim, dim), lambda i: (0, i, 0, 0)), gate, gate),
        compiler_params=params(48), name="delta_grads", cost_estimate=cost(50 * flops, 9),
    )(delta_query, delta_key, delta_value, delta_out_grad, beta_steps, decay_steps,
      mem_in, grad_end, transit, lgrad, inverse, w_all, uv_all, mixing, near)

    slot = pltpu.VMEM((n, 3 * heads, features // n), F32)
    input_grad, sums, dkey, dvalue = pl.pallas_call(
        functools.partial(tail_kernel, n, m, span),
        out_shape=(shape(size, features // m), shape(3 * heads, features // n),
                   shape(size, attn_width), shape(size, attn_width)),
        in_specs=[vmem] * 11,
        out_specs=(vmem,) * 4,
        scratch_shapes=[slot, slot, pltpu.VMEM((m, 2 * heads, size), F32),
                        pltpu.VMEM((span, attn_heads, 8, size), F32),
                        sem((n,)), sem((n,)), sem((m,)), sem((m,)), sem((span,)), sem((span,))],
        compiler_params=params(48, collective_id=1, has_side_effects=True),
        name="tail_exchange", cost_estimate=cost(4 * attn_flops, 6),
    )(layer_input, dbeta.reshape(heads, size), ddecay.reshape(heads, size), betas, decays, slope,
      weight_cols, attn_key, attn_value, qg_all, stats)
    return (dq, dk, dv, boundary, input_grad, sums[:heads], sums[heads:2 * heads],
            sums[2 * heads:, 0], sums[2 * heads:, 1], dquery, dkey, dvalue)


def solution(mesh):
    rows, heads, both = P("seq", None), P("head"), P("seq", "head")
    wide, state = P("head", None), P("head", None, None)
    return jax.shard_map(
        shards,
        mesh=mesh,
        in_specs=(rows, wide, wide, heads, heads, both, both, both, both, state, state,
                  both, both, both, both),
        out_specs=(both, both, both, P("seq", "head", None, None), both, P("head", "seq"),
                   P("head", "seq"), heads, heads, both, both, both),
        check_vma=False,
    )
```

```python
import functools
import math

import jax
import jax.numpy as jnp
from jax import lax
from jax.experimental import pallas as pl
from jax.experimental.pallas import tpu as pltpu
from jax.sharding import PartitionSpec as P

AHD = 128
WINDOW = 1024
HOP_TICKS = 3
EARLY = 3
MESH = pl.DeviceIdType.MESH
F32 = jnp.float32
BF16 = jnp.bfloat16
NN = (((1,), (0,)), ((), ()))
NT = (((1,), (1,)), ((), ()))
TN = (((0,), (0,)), ((), ()))


def parts(value):
    if isinstance(value, tuple):
        return value
    if value.dtype == BF16:
        return (value,)
    high = value.astype(BF16)
    return (high, (value - high.astype(F32)).astype(BF16))


def mul(left, right, dims=NN):
    left, right = parts(left), parts(right)
    total = None
    for i, a in reversed(list(enumerate(left))):
        for j, b in reversed(list(enumerate(right))):
            if i + j < 2:
                term = lax.dot_general(a, b, dims, preferred_element_type=F32)
                total = term if total is None else total + term
    return total


def row_sum(value):
    return jnp.sum(value, axis=1, keepdims=True)


def col_sum(value):
    return jnp.sum(value, axis=0, keepdims=True)


def grids(size):
    rows = lax.broadcasted_iota(jnp.int32, (size, size), 0)
    cols = lax.broadcasted_iota(jnp.int32, (size, size), 1)
    return rows, cols


def as_row(col, rows, cols):
    return col_sum(jnp.where(rows == cols, col, 0.0))


def as_col(row, rows, cols):
    return row_sum(jnp.where(rows == cols, row, 0.0))


def head_terms(q, k, decay_row, rows, cols):
    kf = k.astype(F32)
    qf = q.astype(F32)
    k_norm = lax.rsqrt(row_sum(kf * kf) + 1e-06)
    q_norm = lax.rsqrt(row_sum(qf * qf) + 1e-06)
    rk = k_norm
    rq = q_norm * (1.0 / math.sqrt(q.shape[1]))
    cum = row_sum(jnp.where(cols <= rows, decay_row, 0.0))
    cum_row = as_row(cum, rows, cols)
    lower = rows >= cols
    ratios = jnp.where(lower, jnp.exp(jnp.where(lower, cum - cum_row, 0.0)), 0.0)
    growth = jnp.exp(cum)
    last = row_sum(decay_row)
    tail = jnp.exp(last - cum)
    return kf, qf, k_norm, q_norm, rk, rq, ratios, growth, jnp.exp(last), tail


def local_kernel(q_ref, k_ref, v_ref, do_ref, beta_ref, decay_ref,
                 transit_ref, offset_ref, lgrad_ref, t_ref, w_ref, uv_ref, p_ref, n_ref):
    size = q_ref.shape[0]
    count = beta_ref.shape[1]
    width = q_ref.shape[1] // count
    rows, cols = grids(size)
    inverses, systems, kept = [], [], []
    for j in range(count):
        lanes = slice(j * width, (j + 1) * width)
        q, k = q_ref[:, lanes], k_ref[:, lanes]
        beta, decay = as_col(beta_ref[0, j:j + 1, :], rows, cols), decay_ref[0, j:j + 1, :]
        kf, qf, _, _, rk, rq, ratios, growth, last, tail = head_terms(q, k, decay, rows, cols)
        rk_row = as_row(rk, rows, cols)
        near = jnp.where(rows > cols, ratios * (mul(k, k, NT) * rk * rk_row), 0.0)
        mixing = ratios * (mul(q, k, NT) * rq * rk_row)
        n_ref[j] = near
        p_ref[j] = mixing
        systems.append(beta * near)
        kept.append((kf * rk, qf * rq, beta, growth, last, tail, mixing))
        pair = (rows // 2 == cols // 2) & (rows > cols)
        inverses.append(jnp.where(rows == cols, 1.0, jnp.where(pair, -systems[-1], 0.0)))
    span = 2
    while span < size:
        mask = (rows // (2 * span) == cols // (2 * span)) & (rows // span > cols // span)
        split = [parts(inverse) for inverse in inverses]
        halves = [mul(split[j], jnp.where(mask, systems[j], 0.0)) for j in range(count)]
        inverses = [inverses[j] - mul(halves[j], split[j]) for j in range(count)]
        span *= 2
    for j in range(count):
        lanes = slice(j * width, (j + 1) * width)
        keys, queries, beta, growth, last, tail, mixing = kept[j]
        t_ref[j] = inverses[j]
        split = parts(inverses[j])
        w_all = mul(split, (beta * growth) * keys)
        uv_all = mul(split, beta * v_ref[:, lanes].astype(F32))
        w_ref[j] = w_all
        uv_ref[j] = uv_all
        w_split = parts(w_all)
        tail_keys = parts(keys * tail)
        transit_ref[j] = jnp.where(rows == cols, last, 0.0) - mul(tail_keys, w_split, TN)
        offset_ref[j] = mul(tail_keys, uv_all, TN)
        reach = growth * queries - mul(mixing, w_split)
        lgrad_ref[j] = mul(reach, do_ref[:, lanes], TN)


def meet(n, m, me, head):
    barrier = pltpu.get_barrier_semaphore()
    for d in range(1, n):
        pl.semaphore_signal(barrier, inc=1, device_id=(lax.rem(me + d, n), head),
                            device_id_type=MESH)
    for d in range(1, m):
        pl.semaphore_signal(barrier, inc=1, device_id=(me, lax.rem(head + d, m)),
                            device_id_type=MESH)
    return lambda: pl.semaphore_wait(barrier, n + m - 2)


def remote(src, dst, send, recv, device):
    return pltpu.make_async_remote_copy(src_ref=src, dst_ref=dst, send_sem=send, recv_sem=recv,
                                        device_id=device, device_id_type=MESH)


def relay_kernel(n, m, span, q_ref, k_ref, v_ref, do_ref, beta_ref, decay_ref, init_ref, next_ref,
                 bw_ref, dw_ref, aq_ref, ak_ref, av_ref, ag_ref,
                 transit_ref, lgrad_ref, t_ref, w_ref, uv_ref, p_ref, n_ref, mem_ref, grad_ref,
                 weight_ref, qg_ref, dquery_ref, stat_ref,
                 kv_ref, offset_ref, slices, send_f, recv_f, send_b, recv_b, sf_sem, rf_sem, sb_sem, rb_sem,
                 skv_sem, rkv_sem, sqg_sem, rqg_sem, sw_sem, rw_sem):
    me = lax.axis_index("seq")
    head = lax.axis_index("head")
    heads = init_ref.shape[0]
    steps, group, _ = beta_ref.shape
    right, left = lax.rem(me + 1, n), lax.rem(me + n - 1, n)
    has_left, has_right = me > 0, me < n - 1
    entered = meet(n, m, me, head)
    width = ak_ref.shape[1]
    kv_ref[0, :, :width] = ak_ref[...]
    kv_ref[0, :, width:] = av_ref[...]
    qg_ref[0, :, :width] = aq_ref[...]
    qg_ref[0, :, width:] = ag_ref[...]
    part = bw_ref.shape[1] // m
    for p in range(m):
        lanes = slice(p * part, (p + 1) * part)
        slices[p, :heads] = bw_ref[:, lanes].astype(F32)
        slices[p, heads:] = dw_ref[:, lanes].astype(F32)
    weight_ref[head] = slices[head]
    entered()

    def copy_kv(d):
        return remote(kv_ref.at[0], kv_ref.at[d], skv_sem.at[d], rkv_sem.at[d],
                      (lax.rem(me + d, n), head))

    def copy_qg(d):
        return remote(qg_ref.at[0], qg_ref.at[d], sqg_sem.at[d], rqg_sem.at[d],
                      (lax.rem(me + n - d, n), head))

    def copy_weight(d):
        peer = lax.rem(head + d, m)
        return remote(slices.at[peer], weight_ref.at[head], sw_sem.at[d], rw_sem.at[d], (me, peer))

    def came_weight(d):
        peer = lax.rem(head + m - d, m)
        return remote(slices.at[peer], weight_ref.at[peer], sw_sem.at[d], rw_sem.at[d], (me, peer))

    def start_far(d, now):
        @pl.when(now & (me + d < n))
        def _():
            copy_kv(d).start()

        @pl.when(now & (me >= d))
        def _():
            copy_qg(d).start()

    for d in range(1, m):
        copy_weight(d).start()
    for d in range(1, span):
        if d <= EARLY:
            start_far(d, True)

        @pl.when(me < d)
        def _(d=d):
            kv_ref[d] = jnp.zeros(kv_ref.shape[1:], BF16)

        @pl.when(me + d >= n)
        def _(d=d):
            qg_ref[d] = jnp.zeros(qg_ref.shape[1:], BF16)

    lane_count = q_ref.shape[1] // steps

    def local_step(i):
        lanes = pl.ds(pl.multiple_of(i * lane_count, 128), lane_count)
        mine = pl.ds(i * group, group)
        local_kernel(q_ref.at[:, lanes], k_ref.at[:, lanes], v_ref.at[:, lanes],
                     do_ref.at[:, lanes], beta_ref.at[pl.ds(i, 1)], decay_ref.at[pl.ds(i, 1)],
                     transit_ref.at[mine], offset_ref.at[mine], lgrad_ref.at[mine], t_ref.at[mine],
                     w_ref.at[mine], uv_ref.at[mine], p_ref.at[mine], n_ref.at[mine])

    pace = min(HOP_TICKS, group)
    last_tick = HOP_TICKS * (n - 1) + heads
    begin_late = HOP_TICKS * jnp.maximum(me, n - 1 - me)
    apart = begin_late - HOP_TICKS * jnp.minimum(me, n - 1 - me)
    rows_tick = jnp.where(apart >= heads + 3, begin_late - 4, last_tick)

    def attend():
        for d in range(1, span):
            @pl.when(me >= d)
            def _(d=d):
                copy_kv(d).wait_recv()
        for h in range(width // AHD):
            lanes = slice(h * AHD, (h + 1) * AHD)
            more = slice(width + h * AHD, width + (h + 1) * AHD)
            attn_rows(me, aq_ref.at[:, lanes], ag_ref.at[:, lanes], kv_ref.at[:, :, lanes],
                      kv_ref.at[:, :, more], dquery_ref.at[:, lanes], stat_ref.at[h])

    def copy_f(h):
        return pltpu.make_async_remote_copy(
            src_ref=send_f.at[h], dst_ref=recv_f.at[h], send_sem=sf_sem.at[h],
            recv_sem=rf_sem.at[h], device_id=(right, head), device_id_type=MESH)

    def copy_b(h):
        return pltpu.make_async_remote_copy(
            src_ref=send_b.at[h], dst_ref=recv_b.at[h], send_sem=sb_sem.at[h],
            recv_sem=rb_sem.at[h], device_id=(left, head), device_id_type=MESH)

    def tick(t, carry):
        @pl.when((t % pace == 0) & (t // pace < steps))
        def _():
            local_step(t // pace)

        for d in range(EARLY + 1, span):
            start_far(d, t == HOP_TICKS * (d - EARLY - 1))

        @pl.when(t == rows_tick)
        def _():
            attend()

        hf = t - HOP_TICKS * me
        hb = t - HOP_TICKS * (n - 1 - me)

        @pl.when((hf >= 0) & (hf < heads))
        def _():
            @pl.when(has_left)
            def _():
                copy_f(hf).wait_recv()
                mem_ref[hf] = recv_f[hf]

            @pl.when(jnp.logical_not(has_left))
            def _():
                mem_ref[hf] = init_ref[hf]

            @pl.when(has_right)
            def _():
                send_f[hf] = mul(transit_ref[hf], mem_ref[hf]) + offset_ref[hf]
                copy_f(hf).start()

        @pl.when((hb >= 0) & (hb < heads))
        def _():
            @pl.when(has_right)
            def _():
                copy_b(hb).wait_recv()
                grad_ref[hb] = recv_b[hb]

            @pl.when(jnp.logical_not(has_right))
            def _():
                grad_ref[hb] = next_ref[hb]

            @pl.when(has_left)
            def _():
                send_b[hb] = mul(transit_ref[hb], grad_ref[hb], TN) + lgrad_ref[hb]
                copy_b(hb).start()

        return carry

    lax.fori_loop(0, last_tick + 1, tick, 0)

    def drain(h, carry):
        @pl.when(has_right)
        def _():
            copy_f(h).wait_send()

        @pl.when(has_left)
        def _():
            copy_b(h).wait_send()

        return carry

    lax.fori_loop(0, heads, drain, 0)
    for d in range(1, m):
        came_weight(d).wait_recv()
        copy_weight(d).wait_send()
    for d in range(1, span):
        @pl.when(me + d < n)
        def _(d=d):
            copy_kv(d).wait_send()
            copy_qg(d).wait_recv()

        @pl.when(me >= d)
        def _(d=d):
            copy_qg(d).wait_send()


def grads_kernel(q_ref, k_ref, v_ref, do_ref, beta_ref, decay_ref, mem_ref, grad_ref,
                 transit_ref, lgrad_ref, t_ref, w_ref, uv_ref, p_ref, n_ref,
                 dq_ref, dk_ref, dv_ref, bound_ref, dbeta_ref, ddecay_ref):
    size = q_ref.shape[0]
    count = beta_ref.shape[1]
    width = q_ref.shape[1] // count
    rows, cols = grids(size)
    for j in range(count):
        lanes = slice(j * width, (j + 1) * width)
        q, k, do = q_ref[:, lanes], k_ref[:, lanes], do_ref[:, lanes]
        beta, decay = as_col(beta_ref[0, j:j + 1, :], rows, cols), decay_ref[0, j:j + 1, :]
        kf, qf, k_norm, q_norm, rk, rq, ratios, growth, last, tail = head_terms(
            q, k, decay, rows, cols)
        rk_row = as_row(rk, rows, cols)
        dof = do.astype(F32)
        memory, grad = mem_ref[j], grad_ref[j]
        near, mixing = n_ref[j], p_ref[j]
        mem_s, grad_s = parts(memory), parts(grad)
        updates = uv_ref[j] - mul(w_ref[j], mem_s)
        up_s = parts(updates)
        q_mem = rq * mul(q, mem_s)
        k_mem = rk * mul(k, mem_s)
        dup = mul(mixing, do, TN) + (rk * tail) * mul(k, grad_s)
        drhs = mul(t_ref[j], dup, TN)
        drhs_s = parts(drhs)
        dmix = jnp.where(rows >= cols, mul(do, up_s, NT), 0.0)
        dqk = dmix * ratios
        dsys = jnp.where(rows > cols, -mul(drhs_s, up_s, NT), 0.0)
        dgram = dsys * beta * ratios
        dval = beta * drhs
        dquery = growth * mul(do, mem_s, NT) + mul(dqk * rk_row, k)
        dtail = mul(up_s, grad_s, NT)
        dkey = mul(dqk * rq, q, TN) + dtail * tail
        dkey = dkey - (beta * growth) * mul(drhs_s, mem_s, NT)
        dkey = dkey + mul((dgram + dgram.T) * rk_row, k)
        dbeta = row_sum(drhs * (v_ref[:, lanes].astype(F32) - growth * k_mem))
        dbeta_ref[0, j:j + 1, :] = as_row(dbeta + row_sum(dsys * near), rows, cols)
        inner = dsys * (beta * near) + dmix * mixing
        tails = row_sum(dtail * kf) * (rk * tail)
        dcum = growth * (row_sum(dof * q_mem) - row_sum(dval * k_mem)) - tails + row_sum(inner)
        dcum_row = as_row(dcum, rows, cols) - col_sum(inner)
        at_end = col_sum(tails) + last * col_sum(row_sum(grad * memory))
        after = row_sum(jnp.where(cols >= rows, dcum_row, 0.0)) + at_end
        ddecay_ref[0, j:j + 1, :] = as_row(after, rows, cols)
        dq_ref[:, lanes] = rq * (dquery - qf * (q_norm * q_norm * row_sum(qf * dquery)))
        dk_ref[:, lanes] = rk * (dkey - kf * (k_norm * k_norm * row_sum(kf * dkey)))
        dv_ref[:, lanes] = dval
        bound_ref[0, j] = mul(transit_ref[j], grad_s, TN) + lgrad_ref[j]


def attn_rows(place, q_ref, g_ref, k_ref, v_ref, dq_ref, stat_ref):
    size = q_ref.shape[0]
    count = k_ref.shape[0]
    span = count * size
    scale = 1.0 / math.sqrt(AHD)
    keys = k_ref[...].reshape(span, AHD)
    values = v_ref[...].reshape(span, AHD)
    rows = lax.broadcasted_iota(jnp.int32, (size, span), 0)
    cols = lax.broadcasted_iota(jnp.int32, (size, span), 1)
    back = cols // size
    gap = rows - cols % size + back * size
    allowed = (gap >= 0) & (gap < WINDOW) & (back <= place)
    scores = jnp.where(allowed, mul(q_ref[...], keys, NT) * scale, -1e30)
    top = jnp.max(scores, axis=1, keepdims=True)
    weights = jnp.exp(scores - top)
    inverse = 1.0 / row_sum(weights)
    weights = weights * inverse
    weight_grad = mul(g_ref[...], values, NT)
    row_term = row_sum(weights * weight_grad)
    dscores = weights * (weight_grad - row_term) * scale
    dq_ref[...] = mul(dscores, keys)
    square = grids(size)
    stat_ref[...] = jnp.zeros(stat_ref.shape, F32)
    stat_ref[0:1, :] = as_row(top, *square)
    stat_ref[1:2, :] = as_row(inverse, *square)
    stat_ref[2:3, :] = as_row(row_term, *square)


def tail_kernel(n, m, span, x_ref, dbeta_ref, ddecay_ref, beta_ref, decay_ref, slope_ref,
                weight_ref, ak_ref, av_ref, qg_ref, stat_ref,
                input_ref, wsum_ref, psum_ref, dk_ref, dv_ref,
                terms, arrived, every, stats, sums, sp_sem, rp_sem, st_sem, rt_sem, se_sem, re_sem, ss_sem, rs_sem):
    me = lax.axis_index("seq")
    head = lax.axis_index("head")
    entered = meet(n, m, me, head)
    heads, size = beta_ref.shape
    part = x_ref.shape[1] // n
    betas, ddecay = beta_ref[...], ddecay_ref[...]
    grad_d = ddecay * slope_ref[...]
    every[head, :heads] = dbeta_ref[...] * (betas * (1.0 - betas))
    every[head, heads:] = grad_d
    stats[0] = stat_ref[...]
    lane = lax.broadcasted_iota(jnp.int32, (heads, size), 1)
    sums[0] = jnp.where(lane == 0, row_sum(ddecay * decay_ref[...]),
                        jnp.where(lane == 1, row_sum(grad_d), 0.0))
    mine = parts(every[head])
    entered()

    def copy_stat(d):
        return remote(stats.at[0], stats.at[d], ss_sem.at[d], rs_sem.at[d],
                      (lax.rem(me + n - d, n), head))

    def copy_every(d):
        return remote(every.at[head], every.at[head], se_sem.at[d], re_sem.at[d],
                      (me, lax.rem(head + d, m)))

    def came_every(d):
        peer = lax.rem(head + m - d, m)
        return remote(every.at[peer], every.at[peer], se_sem.at[d], re_sem.at[d], (me, peer))

    def copy_sum(d):
        return remote(sums.at[0], sums.at[d], sp_sem.at[d], rp_sem.at[d],
                      (lax.rem(me + d, n), head))

    def copy_term(d):
        return remote(terms.at[d], arrived.at[d], st_sem.at[d], rt_sem.at[d],
                      (lax.rem(me + d, n), head))

    for d in range(1, span):
        @pl.when(me >= d)
        def _(d=d):
            copy_stat(d).start()

        @pl.when(me + d >= n)
        def _(d=d):
            stats[d] = jnp.zeros(stats.shape[1:], F32)
    for d in range(1, m):
        copy_every(d).start()

    def fill(d):
        place = pl.multiple_of(lax.rem(me + d, n) * part, 128)
        terms[d] = mul(mine, x_ref[:, pl.ds(place, part)])

    def send_term(d, carry):
        fill(d)
        copy_term(d).start()
        copy_sum(d).start()
        return carry

    lax.fori_loop(1, n, send_term, 0)
    fill(0)
    for d in range(1, span):
        @pl.when(me + d < n)
        def _(d=d):
            copy_stat(d).wait_recv()
    scale = 1.0 / math.sqrt(AHD)
    rows, cols = grids(size)
    width = ak_ref.shape[1]
    for h in range(width // AHD):
        lanes = slice(h * AHD, (h + 1) * AHD)
        more = slice(width + h * AHD, width + (h + 1) * AHD)
        key, value = ak_ref[:, lanes], av_ref[:, lanes]
        dkey = dvalue = jnp.zeros((size, AHD), F32)
        for d in range(span):
            query, grad = qg_ref[d, :, lanes], qg_ref[d, :, more]
            gap = cols - rows + d * size
            allowed = (gap >= 0) & (gap < WINDOW)
            scores = mul(key, query, NT) * scale - stats[d, h, 0:1, :]
            weights = jnp.where(allowed, jnp.exp(jnp.where(allowed, scores, 0.0)), 0.0)
            weights = weights * stats[d, h, 1:2, :]
            dscores = weights * (mul(value, grad, NT) - stats[d, h, 2:3, :]) * scale
            dvalue = dvalue + mul(weights, grad)
            dkey = dkey + mul(dscores, query)
        dk_ref[:, lanes] = dkey
        dv_ref[:, lanes] = dvalue
    for d in range(1, m):
        came_every(d).wait_recv()
    left = parts(every[...].reshape(m * 2 * heads, size))
    chunk = next(c for c in (512, 256, 128) if weight_ref.shape[2] % c == 0)
    for c in range(0, weight_ref.shape[2], chunk):
        right = weight_ref[:, :, c:c + chunk].reshape(m * 2 * heads, chunk).astype(BF16)
        input_ref[:, c:c + chunk] = mul(left, right, TN)
    total, total_sum = terms[0], sums[0]
    for d in range(1, n):
        copy_term(d).wait_recv()
        total = total + arrived[d]
        copy_sum(d).wait_recv()
        total_sum = total_sum + sums[d]
    wsum_ref[...] = total
    psum_ref[...] = total_sum
    for d in range(1, span):
        @pl.when(me >= d)
        def _(d=d):
            copy_stat(d).wait_send()
    for d in range(1, m):
        copy_every(d).wait_send()
    for d in range(1, n):
        copy_term(d).wait_send()
        copy_sum(d).wait_send()


def shards(layer_input, beta_weight, decay_weight, log_rate, decay_bias, delta_query, delta_key,
           delta_value, delta_out_grad, state_init, state_grad_next, attn_query, attn_key,
           attn_value, attn_out_grad):
    n, m = lax.axis_size("seq"), lax.axis_size("head")
    me = lax.axis_index("seq")
    size, width = delta_query.shape
    heads = beta_weight.shape[0]
    features = layer_input.shape[1]
    dim = width // heads
    group = next(c for c in (4, 2, 1) if heads % c == 0)
    steps = heads // group
    attn_width = attn_query.shape[1]
    attn_heads = attn_width // AHD
    span = min(-(-WINDOW // size), n - 1) + 1

    betas = jax.nn.sigmoid(lax.dot_general(beta_weight, layer_input, NT, preferred_element_type=F32))
    shifted = lax.dot_general(decay_weight, layer_input, NT, preferred_element_type=F32)
    shifted = shifted + decay_bias[:, None]
    rate = -jnp.exp(log_rate)[:, None]
    decays = rate * jax.nn.softplus(shifted)
    slope = rate * jax.nn.sigmoid(shifted)

    def shape(*dims, kind=F32):
        return jax.ShapeDtypeStruct(dims, kind)

    def params(mib, **more):
        return pltpu.CompilerParams(vmem_limit_bytes=mib * 1024 * 1024, **more)

    def cost(flops, mib):
        return pl.CostEstimate(flops=flops, bytes_accessed=mib << 20, transcendentals=0)

    vmem = pl.BlockSpec(memory_space=pltpu.VMEM)
    state, pair = shape(heads, dim, dim), shape(heads, size, size)
    per_token = shape(heads, size, dim)
    box, sem = pltpu.VMEM((heads, dim, dim), F32), pltpu.SemaphoreType.DMA
    beta_steps = betas.reshape(steps, group, size)
    decay_steps = decays.reshape(steps, group, size)
    flops = 2 * heads * size * size * dim
    (transit, lgrad, inverse, w_all, uv_all, mixing, near, mem_in, grad_end, weight_cols, qg_all,
     dquery, stats) = pl.pallas_call(
        functools.partial(relay_kernel, n, m, span),
        out_shape=(state, state, pair, per_token, per_token, pair, pair, state, state,
                   shape(m, 2 * heads, features // m),
                   shape(span, size, 2 * attn_width, kind=BF16),
                   shape(size, attn_width), shape(attn_heads, 8, size)),
        in_specs=[vmem] * 14,
        out_specs=(vmem,) * 13,
        scratch_shapes=[pltpu.VMEM((span, size, 2 * attn_width), BF16), box, pltpu.VMEM((m, 2 * heads, features // m), F32), box, box, box, box,
                        sem((heads,)), sem((heads,)), sem((heads,)), sem((heads,)),
                        sem((span,)), sem((span,)), sem((span,)), sem((span,)), sem((m,)), sem((m,))],
        compiler_params=params(48, collective_id=0, has_side_effects=True),
        name="state_relay", cost_estimate=cost(66 * flops, 16),
    )(delta_query, delta_key, delta_value, delta_out_grad, beta_steps, decay_steps, state_init,
      state_grad_next, beta_weight, decay_weight, attn_query, attn_key, attn_value, attn_out_grad)

    attn_flops = 2 * size * span * size * attn_width
    tokens = pl.BlockSpec((size, group * dim), lambda i: (0, i))
    gate = pl.BlockSpec((1, group, size), lambda i: (i, 0, 0))
    square = pl.BlockSpec((group, dim, dim), lambda i: (i, 0, 0))
    pairs = pl.BlockSpec((group, size, size), lambda i: (i, 0, 0))
    token_rows = pl.BlockSpec((group, size, dim), lambda i: (i, 0, 0))
    flat, gate_out = shape(size, width), shape(steps, group, size)
    dq, dk, dv, boundary, dbeta, ddecay = pl.pallas_call(
        grads_kernel,
        grid=(steps,),
        out_shape=(flat, flat, flat, shape(1, heads, dim, dim), gate_out, gate_out),
        in_specs=[tokens] * 4 + [gate] * 2 + [square] * 4 + [pairs, token_rows, token_rows, pairs, pairs],
        out_specs=(tokens, tokens, tokens,
                   pl.BlockSpec((1, group, dim, dim), lambda i: (0, i, 0, 0)), gate, gate),
        compiler_params=params(48), name="delta_grads", cost_estimate=cost(50 * flops, 9),
    )(delta_query, delta_key, delta_value, delta_out_grad, beta_steps, decay_steps,
      mem_in, grad_end, transit, lgrad, inverse, w_all, uv_all, mixing, near)

    slot = pltpu.VMEM((n, 2 * heads, features // n), F32)
    input_grad, weights_grad, sums, dkey, dvalue = pl.pallas_call(
        functools.partial(tail_kernel, n, m, span),
        out_shape=(shape(size, features // m), shape(2 * heads, features // n), shape(heads, size),
                   shape(size, attn_width), shape(size, attn_width)),
        in_specs=[vmem] * 11,
        out_specs=(vmem,) * 5,
        scratch_shapes=[slot, slot, pltpu.VMEM((m, 2 * heads, size), F32),
                        pltpu.VMEM((span, attn_heads, 8, size), F32),
                        pltpu.VMEM((n, heads, size), F32), sem((n,)), sem((n,)),
                        sem((n,)), sem((n,)), sem((m,)), sem((m,)), sem((span,)), sem((span,))],
        compiler_params=params(48, collective_id=1, has_side_effects=True),
        name="tail_exchange", cost_estimate=cost(4 * attn_flops, 6),
    )(layer_input, dbeta.reshape(heads, size), ddecay.reshape(heads, size), betas, decays, slope,
      weight_cols, attn_key, attn_value, qg_all, stats)
    return (dq, dk, dv, boundary, input_grad, weights_grad[:heads], weights_grad[heads:],
            sums[:, 0], sums[:, 1], dquery, dkey, dvalue)


def solution(mesh):
    rows, heads, both = P("seq", None), P("head"), P("seq", "head")
    wide, state = P("head", None), P("head", None, None)
    return jax.shard_map(
        shards,
        mesh=mesh,
        in_specs=(rows, wide, wide, heads, heads, both, both, both, both, state, state,
                  both, both, both, both),
        out_specs=(both, both, both, P("seq", "head", None, None), both, P("head", "seq"),
                   P("head", "seq"), heads, heads, both, both, both),
        check_vma=False,
    )
```

```python
import functools
import math

import jax
import jax.numpy as jnp
from jax import lax
from jax.experimental import pallas as pl
from jax.experimental.pallas import tpu as pltpu
from jax.sharding import PartitionSpec as P

AHD = 128
WINDOW = 1024
HOP_TICKS = 2
EARLY = 3
MESH = pl.DeviceIdType.MESH
F32 = jnp.float32
BF16 = jnp.bfloat16
NN = (((1,), (0,)), ((), ()))
NT = (((1,), (1,)), ((), ()))
TN = (((0,), (0,)), ((), ()))


def parts(value):
    if isinstance(value, tuple):
        return value
    if value.dtype == BF16:
        return (value,)
    high = value.astype(BF16)
    return (high, (value - high.astype(F32)).astype(BF16))


def mul(left, right, dims=NN):
    left, right = parts(left), parts(right)
    total = None
    for i, a in reversed(list(enumerate(left))):
        for j, b in reversed(list(enumerate(right))):
            if i + j < 2:
                term = lax.dot_general(a, b, dims, preferred_element_type=F32)
                total = term if total is None else total + term
    return total


def row_sum(value):
    return jnp.sum(value, axis=1, keepdims=True)


def col_sum(value):
    return jnp.sum(value, axis=0, keepdims=True)


def grids(size):
    rows = lax.broadcasted_iota(jnp.int32, (size, size), 0)
    cols = lax.broadcasted_iota(jnp.int32, (size, size), 1)
    return rows, cols


def as_row(col, rows, cols):
    return col_sum(jnp.where(rows == cols, col, 0.0))


def as_col(row, rows, cols):
    return row_sum(jnp.where(rows == cols, row, 0.0))


def head_terms(q, k, decay_row, rows, cols):
    kf = k.astype(F32)
    qf = q.astype(F32)
    k_norm = lax.rsqrt(row_sum(kf * kf) + 1e-06)
    q_norm = lax.rsqrt(row_sum(qf * qf) + 1e-06)
    rk = k_norm
    rq = q_norm * (1.0 / math.sqrt(q.shape[1]))
    cum = row_sum(jnp.where(cols <= rows, decay_row, 0.0))
    cum_row = as_row(cum, rows, cols)
    lower = rows >= cols
    ratios = jnp.where(lower, jnp.exp(jnp.where(lower, cum - cum_row, 0.0)), 0.0)
    growth = jnp.exp(cum)
    last = row_sum(decay_row)
    tail = jnp.exp(last - cum)
    return kf, qf, k_norm, q_norm, rk, rq, ratios, growth, jnp.exp(last), tail


def local_kernel(q_ref, k_ref, v_ref, do_ref, beta_ref, decay_ref,
                 transit_ref, offset_ref, lgrad_ref, t_ref, w_ref, uv_ref, p_ref, n_ref):
    size = q_ref.shape[0]
    count = beta_ref.shape[1]
    width = q_ref.shape[1] // count
    rows, cols = grids(size)
    inverses, systems, kept = [], [], []
    for j in range(count):
        lanes = slice(j * width, (j + 1) * width)
        q, k = q_ref[:, lanes], k_ref[:, lanes]
        beta, decay = as_col(beta_ref[0, j:j + 1, :], rows, cols), decay_ref[0, j:j + 1, :]
        kf, qf, _, _, rk, rq, ratios, growth, last, tail = head_terms(q, k, decay, rows, cols)
        rk_row = as_row(rk, rows, cols)
        near = jnp.where(rows > cols, ratios * (mul(k, k, NT) * rk * rk_row), 0.0)
        mixing = ratios * (mul(q, k, NT) * rq * rk_row)
        n_ref[j] = near
        p_ref[j] = mixing
        systems.append(beta * near)
        kept.append((kf * rk, qf * rq, beta, growth, last, tail, mixing))
        pair = (rows // 2 == cols // 2) & (rows > cols)
        inverses.append(jnp.where(rows == cols, 1.0, jnp.where(pair, -systems[-1], 0.0)))
    span = 2
    while span < size:
        mask = (rows // (2 * span) == cols // (2 * span)) & (rows // span > cols // span)
        split = [parts(inverse) for inverse in inverses]
        halves = [mul(split[j], jnp.where(mask, systems[j], 0.0)) for j in range(count)]
        inverses = [inverses[j] - mul(halves[j], split[j]) for j in range(count)]
        span *= 2
    for j in range(count):
        lanes = slice(j * width, (j + 1) * width)
        keys, queries, beta, growth, last, tail, mixing = kept[j]
        t_ref[j] = inverses[j]
        split = parts(inverses[j])
        w_all = mul(split, (beta * growth) * keys)
        uv_all = mul(split, beta * v_ref[:, lanes].astype(F32))
        w_ref[j] = w_all
        uv_ref[j] = uv_all
        w_split = parts(w_all)
        tail_keys = parts(keys * tail)
        transit_ref[j] = jnp.where(rows == cols, last, 0.0) - mul(tail_keys, w_split, TN)
        offset_ref[j] = mul(tail_keys, uv_all, TN)
        reach = growth * queries - mul(mixing, w_split)
        lgrad_ref[j] = mul(reach, do_ref[:, lanes], TN)


def meet(n, m, me, head):
    barrier = pltpu.get_barrier_semaphore()
    for d in range(1, n):
        pl.semaphore_signal(barrier, inc=1, device_id=(lax.rem(me + d, n), head),
                            device_id_type=MESH)
    for d in range(1, m):
        pl.semaphore_signal(barrier, inc=1, device_id=(me, lax.rem(head + d, m)),
                            device_id_type=MESH)
    return lambda: pl.semaphore_wait(barrier, n + m - 2)


def remote(src, dst, send, recv, device):
    return pltpu.make_async_remote_copy(src_ref=src, dst_ref=dst, send_sem=send, recv_sem=recv,
                                        device_id=device, device_id_type=MESH)


def relay_kernel(n, m, span, q_ref, k_ref, v_ref, do_ref, beta_ref, decay_ref, init_ref, next_ref,
                 bw_ref, dw_ref, aq_ref, ak_ref, av_ref, ag_ref,
                 transit_ref, lgrad_ref, t_ref, w_ref, uv_ref, p_ref, n_ref, mem_ref, grad_ref,
                 weight_ref, qg_ref, dquery_ref, stat_ref,
                 kv_ref, offset_ref, slices, send_f, recv_f, send_b, recv_b, sf_sem, rf_sem, sb_sem, rb_sem,
                 skv_sem, rkv_sem, sqg_sem, rqg_sem, sw_sem, rw_sem):
    me = lax.axis_index("seq")
    head = lax.axis_index("head")
    heads = init_ref.shape[0]
    steps, group, _ = beta_ref.shape
    right, left = lax.rem(me + 1, n), lax.rem(me + n - 1, n)
    has_left, has_right = me > 0, me < n - 1
    entered = meet(n, m, me, head)
    width = ak_ref.shape[1]
    kv_ref[0, :, :width] = ak_ref[...]
    kv_ref[0, :, width:] = av_ref[...]
    qg_ref[0, :, :width] = aq_ref[...]
    qg_ref[0, :, width:] = ag_ref[...]
    part = bw_ref.shape[1] // m
    for p in range(m):
        lanes = slice(p * part, (p + 1) * part)
        slices[p, :heads] = bw_ref[:, lanes].astype(F32)
        slices[p, heads:] = dw_ref[:, lanes].astype(F32)
    weight_ref[head] = slices[head]
    entered()

    def copy_kv(d):
        return remote(kv_ref.at[0], kv_ref.at[d], skv_sem.at[d], rkv_sem.at[d],
                      (lax.rem(me + d, n), head))

    def copy_qg(d):
        return remote(qg_ref.at[0], qg_ref.at[d], sqg_sem.at[d], rqg_sem.at[d],
                      (lax.rem(me + n - d, n), head))

    def copy_weight(d):
        peer = lax.rem(head + d, m)
        return remote(slices.at[peer], weight_ref.at[head], sw_sem.at[d], rw_sem.at[d], (me, peer))

    def came_weight(d):
        peer = lax.rem(head + m - d, m)
        return remote(slices.at[peer], weight_ref.at[peer], sw_sem.at[d], rw_sem.at[d], (me, peer))

    def start_far(d, now):
        @pl.when(now & (me + d < n))
        def _():
            copy_kv(d).start()

        @pl.when(now & (me >= d))
        def _():
            copy_qg(d).start()

    for d in range(1, m):
        copy_weight(d).start()
    for d in range(1, span):
        if d <= EARLY:
            start_far(d, True)

        @pl.when(me < d)
        def _(d=d):
            kv_ref[d] = jnp.zeros(kv_ref.shape[1:], BF16)

        @pl.when(me + d >= n)
        def _(d=d):
            qg_ref[d] = jnp.zeros(qg_ref.shape[1:], BF16)

    lane_count = q_ref.shape[1] // steps

    def local_step(i):
        lanes = pl.ds(pl.multiple_of(i * lane_count, 128), lane_count)
        mine = pl.ds(i * group, group)
        local_kernel(q_ref.at[:, lanes], k_ref.at[:, lanes], v_ref.at[:, lanes],
                     do_ref.at[:, lanes], beta_ref.at[pl.ds(i, 1)], decay_ref.at[pl.ds(i, 1)],
                     transit_ref.at[mine], offset_ref.at[mine], lgrad_ref.at[mine], t_ref.at[mine],
                     w_ref.at[mine], uv_ref.at[mine], p_ref.at[mine], n_ref.at[mine])

    pace = min(HOP_TICKS, group)
    last_tick = HOP_TICKS * (n - 1) + heads
    begin_late = HOP_TICKS * jnp.maximum(me, n - 1 - me)
    apart = begin_late - HOP_TICKS * jnp.minimum(me, n - 1 - me)
    rows_tick = jnp.where(apart >= heads + 3, begin_late - 4, last_tick)

    def attend():
        for d in range(1, span):
            @pl.when(me >= d)
            def _(d=d):
                copy_kv(d).wait_recv()
        for h in range(width // AHD):
            lanes = slice(h * AHD, (h + 1) * AHD)
            more = slice(width + h * AHD, width + (h + 1) * AHD)
            attn_rows(me, aq_ref.at[:, lanes], ag_ref.at[:, lanes], kv_ref.at[:, :, lanes],
                      kv_ref.at[:, :, more], dquery_ref.at[:, lanes], stat_ref.at[h])

    def copy_f(h):
        return pltpu.make_async_remote_copy(
            src_ref=send_f.at[h], dst_ref=recv_f.at[h], send_sem=sf_sem.at[h],
            recv_sem=rf_sem.at[h], device_id=(right, head), device_id_type=MESH)

    def copy_b(h):
        return pltpu.make_async_remote_copy(
            src_ref=send_b.at[h], dst_ref=recv_b.at[h], send_sem=sb_sem.at[h],
            recv_sem=rb_sem.at[h], device_id=(left, head), device_id_type=MESH)

    def tick(t, carry):
        @pl.when((t % pace == 0) & (t // pace < steps))
        def _():
            local_step(t // pace)

        for d in range(EARLY + 1, span):
            start_far(d, t == HOP_TICKS * (d - EARLY - 1))

        @pl.when(t == rows_tick)
        def _():
            attend()

        hf = t - HOP_TICKS * me
        hb = t - HOP_TICKS * (n - 1 - me)

        @pl.when((hf >= 0) & (hf < heads))
        def _():
            @pl.when(has_left)
            def _():
                copy_f(hf).wait_recv()
                mem_ref[hf] = recv_f[hf]

            @pl.when(jnp.logical_not(has_left))
            def _():
                mem_ref[hf] = init_ref[hf]

            @pl.when(has_right)
            def _():
                send_f[hf] = mul(transit_ref[hf], mem_ref[hf]) + offset_ref[hf]
                copy_f(hf).start()

        @pl.when((hb >= 0) & (hb < heads))
        def _():
            @pl.when(has_right)
            def _():
                copy_b(hb).wait_recv()
                grad_ref[hb] = recv_b[hb]

            @pl.when(jnp.logical_not(has_right))
            def _():
                grad_ref[hb] = next_ref[hb]

            @pl.when(has_left)
            def _():
                send_b[hb] = mul(transit_ref[hb], grad_ref[hb], TN) + lgrad_ref[hb]
                copy_b(hb).start()

        return carry

    lax.fori_loop(0, last_tick + 1, tick, 0)

    def drain(h, carry):
        @pl.when(has_right)
        def _():
            copy_f(h).wait_send()

        @pl.when(has_left)
        def _():
            copy_b(h).wait_send()

        return carry

    lax.fori_loop(0, heads, drain, 0)
    for d in range(1, m):
        came_weight(d).wait_recv()
        copy_weight(d).wait_send()
    for d in range(1, span):
        @pl.when(me + d < n)
        def _(d=d):
            copy_kv(d).wait_send()
            copy_qg(d).wait_recv()

        @pl.when(me >= d)
        def _(d=d):
            copy_qg(d).wait_send()


def grads_kernel(q_ref, k_ref, v_ref, do_ref, beta_ref, decay_ref, mem_ref, grad_ref,
                 transit_ref, lgrad_ref, t_ref, w_ref, uv_ref, p_ref, n_ref,
                 dq_ref, dk_ref, dv_ref, bound_ref, dbeta_ref, ddecay_ref):
    size = q_ref.shape[0]
    count = beta_ref.shape[1]
    width = q_ref.shape[1] // count
    rows, cols = grids(size)
    for j in range(count):
        lanes = slice(j * width, (j + 1) * width)
        q, k, do = q_ref[:, lanes], k_ref[:, lanes], do_ref[:, lanes]
        beta, decay = as_col(beta_ref[0, j:j + 1, :], rows, cols), decay_ref[0, j:j + 1, :]
        kf, qf, k_norm, q_norm, rk, rq, ratios, growth, last, tail = head_terms(
            q, k, decay, rows, cols)
        rk_row = as_row(rk, rows, cols)
        dof = do.astype(F32)
        memory, grad = mem_ref[j], grad_ref[j]
        near, mixing = n_ref[j], p_ref[j]
        mem_s, grad_s = parts(memory), parts(grad)
        updates = uv_ref[j] - mul(w_ref[j], mem_s)
        up_s = parts(updates)
        q_mem = rq * mul(q, mem_s)
        k_mem = rk * mul(k, mem_s)
        dup = mul(mixing, do, TN) + (rk * tail) * mul(k, grad_s)
        drhs = mul(t_ref[j], dup, TN)
        drhs_s = parts(drhs)
        dmix = jnp.where(rows >= cols, mul(do, up_s, NT), 0.0)
        dqk = dmix * ratios
        dsys = jnp.where(rows > cols, -mul(drhs_s, up_s, NT), 0.0)
        dgram = dsys * beta * ratios
        dval = beta * drhs
        dquery = growth * mul(do, mem_s, NT) + mul(dqk * rk_row, k)
        dtail = mul(up_s, grad_s, NT)
        dkey = mul(dqk * rq, q, TN) + dtail * tail
        dkey = dkey - (beta * growth) * mul(drhs_s, mem_s, NT)
        dkey = dkey + mul((dgram + dgram.T) * rk_row, k)
        dbeta = row_sum(drhs * (v_ref[:, lanes].astype(F32) - growth * k_mem))
        dbeta_ref[0, j:j + 1, :] = as_row(dbeta + row_sum(dsys * near), rows, cols)
        inner = dsys * (beta * near) + dmix * mixing
        tails = row_sum(dtail * kf) * (rk * tail)
        dcum = growth * (row_sum(dof * q_mem) - row_sum(dval * k_mem)) - tails + row_sum(inner)
        dcum_row = as_row(dcum, rows, cols) - col_sum(inner)
        at_end = col_sum(tails) + last * col_sum(row_sum(grad * memory))
        after = row_sum(jnp.where(cols >= rows, dcum_row, 0.0)) + at_end
        ddecay_ref[0, j:j + 1, :] = as_row(after, rows, cols)
        dq_ref[:, lanes] = rq * (dquery - qf * (q_norm * q_norm * row_sum(qf * dquery)))
        dk_ref[:, lanes] = rk * (dkey - kf * (k_norm * k_norm * row_sum(kf * dkey)))
        dv_ref[:, lanes] = dval
        bound_ref[0, j] = mul(transit_ref[j], grad_s, TN) + lgrad_ref[j]


def attn_rows(place, q_ref, g_ref, k_ref, v_ref, dq_ref, stat_ref):
    size = q_ref.shape[0]
    count = k_ref.shape[0]
    span = count * size
    scale = 1.0 / math.sqrt(AHD)
    keys = k_ref[...].reshape(span, AHD)
    values = v_ref[...].reshape(span, AHD)
    rows = lax.broadcasted_iota(jnp.int32, (size, span), 0)
    cols = lax.broadcasted_iota(jnp.int32, (size, span), 1)
    back = cols // size
    gap = rows - cols % size + back * size
    allowed = (gap >= 0) & (gap < WINDOW) & (back <= place)
    scores = jnp.where(allowed, mul(q_ref[...], keys, NT) * scale, -1e30)
    top = jnp.max(scores, axis=1, keepdims=True)
    weights = jnp.exp(scores - top)
    inverse = 1.0 / row_sum(weights)
    weights = weights * inverse
    weight_grad = mul(g_ref[...], values, NT)
    row_term = row_sum(weights * weight_grad)
    dscores = weights * (weight_grad - row_term) * scale
    dq_ref[...] = mul(dscores, keys)
    square = grids(size)
    stat_ref[...] = jnp.zeros(stat_ref.shape, F32)
    stat_ref[0:1, :] = as_row(top, *square)
    stat_ref[1:2, :] = as_row(inverse, *square)
    stat_ref[2:3, :] = as_row(row_term, *square)


def tail_kernel(n, m, span, x_ref, dbeta_ref, ddecay_ref, beta_ref, decay_ref, slope_ref,
                weight_ref, ak_ref, av_ref, qg_ref, stat_ref,
                input_ref, wsum_ref, psum_ref, dk_ref, dv_ref,
                terms, arrived, every, stats, sums, sp_sem, rp_sem, st_sem, rt_sem, se_sem, re_sem, ss_sem, rs_sem):
    me = lax.axis_index("seq")
    head = lax.axis_index("head")
    entered = meet(n, m, me, head)
    heads, size = beta_ref.shape
    part = x_ref.shape[1] // n
    betas, ddecay = beta_ref[...], ddecay_ref[...]
    grad_d = ddecay * slope_ref[...]
    every[head, :heads] = dbeta_ref[...] * (betas * (1.0 - betas))
    every[head, heads:] = grad_d
    stats[0] = stat_ref[...]
    lane = lax.broadcasted_iota(jnp.int32, (heads, size), 1)
    sums[0] = jnp.where(lane == 0, row_sum(ddecay * decay_ref[...]),
                        jnp.where(lane == 1, row_sum(grad_d), 0.0))
    mine = parts(every[head])
    entered()

    def copy_stat(d):
        return remote(stats.at[0], stats.at[d], ss_sem.at[d], rs_sem.at[d],
                      (lax.rem(me + n - d, n), head))

    def copy_every(d):
        return remote(every.at[head], every.at[head], se_sem.at[d], re_sem.at[d],
                      (me, lax.rem(head + d, m)))

    def came_every(d):
        peer = lax.rem(head + m - d, m)
        return remote(every.at[peer], every.at[peer], se_sem.at[d], re_sem.at[d], (me, peer))

    def copy_sum(d):
        return remote(sums.at[0], sums.at[d], sp_sem.at[d], rp_sem.at[d],
                      (lax.rem(me + d, n), head))

    def copy_term(d):
        return remote(terms.at[d], arrived.at[d], st_sem.at[d], rt_sem.at[d],
                      (lax.rem(me + d, n), head))

    for d in range(1, span):
        @pl.when(me >= d)
        def _(d=d):
            copy_stat(d).start()

        @pl.when(me + d >= n)
        def _(d=d):
            stats[d] = jnp.zeros(stats.shape[1:], F32)
    for d in range(1, m):
        copy_every(d).start()

    def fill(d):
        place = pl.multiple_of(lax.rem(me + d, n) * part, 128)
        terms[d] = mul(mine, x_ref[:, pl.ds(place, part)])

    def send_term(d, carry):
        fill(d)
        copy_term(d).start()
        copy_sum(d).start()
        return carry

    lax.fori_loop(1, n, send_term, 0)
    fill(0)
    for d in range(1, span):
        @pl.when(me + d < n)
        def _(d=d):
            copy_stat(d).wait_recv()
    scale = 1.0 / math.sqrt(AHD)
    rows, cols = grids(size)
    width = ak_ref.shape[1]
    for h in range(width // AHD):
        lanes = slice(h * AHD, (h + 1) * AHD)
        more = slice(width + h * AHD, width + (h + 1) * AHD)
        key, value = ak_ref[:, lanes], av_ref[:, lanes]
        dkey = dvalue = jnp.zeros((size, AHD), F32)
        for d in range(span):
            query, grad = qg_ref[d, :, lanes], qg_ref[d, :, more]
            gap = cols - rows + d * size
            allowed = (gap >= 0) & (gap < WINDOW)
            scores = mul(key, query, NT) * scale - stats[d, h, 0:1, :]
            weights = jnp.where(allowed, jnp.exp(jnp.where(allowed, scores, 0.0)), 0.0)
            weights = weights * stats[d, h, 1:2, :]
            dscores = weights * (mul(value, grad, NT) - stats[d, h, 2:3, :]) * scale
            dvalue = dvalue + mul(weights, grad)
            dkey = dkey + mul(dscores, query)
        dk_ref[:, lanes] = dkey
        dv_ref[:, lanes] = dvalue
    for d in range(1, m):
        came_every(d).wait_recv()
    left = parts(every[...].reshape(m * 2 * heads, size))
    chunk = next(c for c in (512, 256, 128) if weight_ref.shape[2] % c == 0)
    for c in range(0, weight_ref.shape[2], chunk):
        right = weight_ref[:, :, c:c + chunk].reshape(m * 2 * heads, chunk).astype(BF16)
        input_ref[:, c:c + chunk] = mul(left, right, TN)
    total, total_sum = terms[0], sums[0]
    for d in range(1, n):
        copy_term(d).wait_recv()
        total = total + arrived[d]
        copy_sum(d).wait_recv()
        total_sum = total_sum + sums[d]
    wsum_ref[...] = total
    psum_ref[...] = total_sum
    for d in range(1, span):
        @pl.when(me >= d)
        def _(d=d):
            copy_stat(d).wait_send()
    for d in range(1, m):
        copy_every(d).wait_send()
    for d in range(1, n):
        copy_term(d).wait_send()
        copy_sum(d).wait_send()


def shards(layer_input, beta_weight, decay_weight, log_rate, decay_bias, delta_query, delta_key,
           delta_value, delta_out_grad, state_init, state_grad_next, attn_query, attn_key,
           attn_value, attn_out_grad):
    n, m = lax.axis_size("seq"), lax.axis_size("head")
    me = lax.axis_index("seq")
    size, width = delta_query.shape
    heads = beta_weight.shape[0]
    features = layer_input.shape[1]
    dim = width // heads
    group = next(c for c in (4, 2, 1) if heads % c == 0)
    steps = heads // group
    attn_width = attn_query.shape[1]
    attn_heads = attn_width // AHD
    span = min(-(-WINDOW // size), n - 1) + 1

    betas = jax.nn.sigmoid(lax.dot_general(beta_weight, layer_input, NT, preferred_element_type=F32))
    shifted = lax.dot_general(decay_weight, layer_input, NT, preferred_element_type=F32)
    shifted = shifted + decay_bias[:, None]
    rate = -jnp.exp(log_rate)[:, None]
    decays = rate * jax.nn.softplus(shifted)
    slope = rate * jax.nn.sigmoid(shifted)

    def shape(*dims, kind=F32):
        return jax.ShapeDtypeStruct(dims, kind)

    def params(mib, **more):
        return pltpu.CompilerParams(vmem_limit_bytes=mib * 1024 * 1024, **more)

    def cost(flops, mib):
        return pl.CostEstimate(flops=flops, bytes_accessed=mib << 20, transcendentals=0)

    vmem = pl.BlockSpec(memory_space=pltpu.VMEM)
    state, pair = shape(heads, dim, dim), shape(heads, size, size)
    per_token = shape(heads, size, dim)
    box, sem = pltpu.VMEM((heads, dim, dim), F32), pltpu.SemaphoreType.DMA
    beta_steps = betas.reshape(steps, group, size)
    decay_steps = decays.reshape(steps, group, size)
    flops = 2 * heads * size * size * dim
    (transit, lgrad, inverse, w_all, uv_all, mixing, near, mem_in, grad_end, weight_cols, qg_all,
     dquery, stats) = pl.pallas_call(
        functools.partial(relay_kernel, n, m, span),
        out_shape=(state, state, pair, per_token, per_token, pair, pair, state, state,
                   shape(m, 2 * heads, features // m),
                   shape(span, size, 2 * attn_width, kind=BF16),
                   shape(size, attn_width), shape(attn_heads, 8, size)),
        in_specs=[vmem] * 14,
        out_specs=(vmem,) * 13,
        scratch_shapes=[pltpu.VMEM((span, size, 2 * attn_width), BF16), box, pltpu.VMEM((m, 2 * heads, features // m), F32), box, box, box, box,
                        sem((heads,)), sem((heads,)), sem((heads,)), sem((heads,)),
                        sem((span,)), sem((span,)), sem((span,)), sem((span,)), sem((m,)), sem((m,))],
        compiler_params=params(48, collective_id=0, has_side_effects=True),
        name="state_relay", cost_estimate=cost(66 * flops, 16),
    )(delta_query, delta_key, delta_value, delta_out_grad, beta_steps, decay_steps, state_init,
      state_grad_next, beta_weight, decay_weight, attn_query, attn_key, attn_value, attn_out_grad)

    attn_flops = 2 * size * span * size * attn_width
    tokens = pl.BlockSpec((size, group * dim), lambda i: (0, i))
    gate = pl.BlockSpec((1, group, size), lambda i: (i, 0, 0))
    square = pl.BlockSpec((group, dim, dim), lambda i: (i, 0, 0))
    pairs = pl.BlockSpec((group, size, size), lambda i: (i, 0, 0))
    token_rows = pl.BlockSpec((group, size, dim), lambda i: (i, 0, 0))
    flat, gate_out = shape(size, width), shape(steps, group, size)
    dq, dk, dv, boundary, dbeta, ddecay = pl.pallas_call(
        grads_kernel,
        grid=(steps,),
        out_shape=(flat, flat, flat, shape(1, heads, dim, dim), gate_out, gate_out),
        in_specs=[tokens] * 4 + [gate] * 2 + [square] * 4 + [pairs, token_rows, token_rows, pairs, pairs],
        out_specs=(tokens, tokens, tokens,
                   pl.BlockSpec((1, group, dim, dim), lambda i: (0, i, 0, 0)), gate, gate),
        compiler_params=params(48), name="delta_grads", cost_estimate=cost(50 * flops, 9),
    )(delta_query, delta_key, delta_value, delta_out_grad, beta_steps, decay_steps,
      mem_in, grad_end, transit, lgrad, inverse, w_all, uv_all, mixing, near)

    slot = pltpu.VMEM((n, 2 * heads, features // n), F32)
    input_grad, weights_grad, sums, dkey, dvalue = pl.pallas_call(
        functools.partial(tail_kernel, n, m, span),
        out_shape=(shape(size, features // m), shape(2 * heads, features // n), shape(heads, size),
                   shape(size, attn_width), shape(size, attn_width)),
        in_specs=[vmem] * 11,
        out_specs=(vmem,) * 5,
        scratch_shapes=[slot, slot, pltpu.VMEM((m, 2 * heads, size), F32),
                        pltpu.VMEM((span, attn_heads, 8, size), F32),
                        pltpu.VMEM((n, heads, size), F32), sem((n,)), sem((n,)),
                        sem((n,)), sem((n,)), sem((m,)), sem((m,)), sem((span,)), sem((span,))],
        compiler_params=params(48, collective_id=1, has_side_effects=True),
        name="tail_exchange", cost_estimate=cost(4 * attn_flops, 6),
    )(layer_input, dbeta.reshape(heads, size), ddecay.reshape(heads, size), betas, decays, slope,
      weight_cols, attn_key, attn_value, qg_all, stats)
    return (dq, dk, dv, boundary, input_grad, weights_grad[:heads], weights_grad[heads:],
            sums[:, 0], sums[:, 1], dquery, dkey, dvalue)


def solution(mesh):
    rows, heads, both = P("seq", None), P("head"), P("seq", "head")
    wide, state = P("head", None), P("head", None, None)
    return jax.shard_map(
        shards,
        mesh=mesh,
        in_specs=(rows, wide, wide, heads, heads, both, both, both, both, state, state,
                  both, both, both, both),
        out_specs=(both, both, both, P("seq", "head", None, None), both, P("head", "seq"),
                   P("head", "seq"), heads, heads, both, both, both),
        check_vma=False,
    )
```
